512 devices in a mesh: dp: 4 (over x), ctx: 32 (over z, core), head: 4 (over y).
Axes of the slice: x: 4, y: 4, z: 16, core: 2. Of those that a mesh axis runs over, the one named last changes fastest.
Arguments:
- tokens: bfloat16 [32768, 4096], P(('dp', 'ctx'), 'head'), parts along dimension 0, may hold values from -6 to 6
- query: bfloat16 [32768, 2048], P(('dp', 'ctx'), 'head'), parts along dimension 0, may hold values from -109 to 109, as said below
- w_key: bfloat16 [4096, 512], P(None, 'head'), may hold values from -0.09375 to 0.09375
- w_value: bfloat16 [4096, 512], P(None, 'head'), may hold values from -0.09375 to 0.09375
- doc_lengths: int32 [64], P('dp'), parts along dimension 0, may hold values from 1 to 2048, 8192 in all
- balance: int32 [128, 32], P('dp'), parts along dimension 0, may hold values from 0 to 31, each once within a row
Outputs:
- attended: bfloat16 [32768, 2048], P(('dp', 'ctx'), 'head'), parts along dimension 0
The draws below stay inside these ranges and needn't reach their ends.
There are 4 independent parts, one for each index of `dp`. The reference program is written for one: setup_inputs(seed, part) draws one part's arguments, and reference() takes and returns one part's arrays. A program takes and returns all parts, laid end to end along the dimension named above; an argument that names none is the same for every part. Nothing has to cross between parts.
Inputs may be any that keep to these rules, and one draw needn't show every extreme that they name: `query`: rows scale the draw independently.
All inputs are finite; a program needn't handle non-finite values.
Results may differ from the reference program's by a relative error of at most 0.012.
The reference program's roundings to bfloat16 on the way count: a program that leaves them out, or rounds other values in their place, can miss the bound.
Values may be sent and summed in bfloat16 or wider, within the bound.
A program may use at most 64 MiB of HBM per device.

```python
import math
import jax
import jax.numpy as jnp
import numpy as np
from jax import lax

D = 4096
HD = 128
QH = 16
KVH = 4
TOK_DEV = 256
NDOCS = 16
SEQ = 8192
BROW = 8
L_MAX = 2048
N_CTX = 32


def draw_query(key, part):
    key = jax.random.fold_in(key, 11)
    first, second = jax.random.split(key)
    scales = jnp.exp(jax.random.uniform(first, (SEQ, 1), jnp.float32, math.log(0.5), math.log(2.0)))
    base = jnp.clip(jax.random.normal(second, (SEQ, QH * HD), jnp.float32), -6.0, 6.0)
    return (base * scales).astype(jnp.bfloat16)


def level_of(rng, extent, pieces, low, top_value):
    def one(dim, blocks):
        steps = jax.random.uniform(jax.random.fold_in(jax.random.fold_in(rng, 6), dim), (blocks,), jnp.float32, low / len(pieces), top_value / len(pieces))
        return jnp.repeat(jnp.exp(steps), extent[dim] // blocks).reshape((-1,) + (1,) * (len(extent) - dim - 1))

    loudness = one(*pieces[0])
    for cut in pieces[1:]:
        loudness = loudness * one(*cut)
    return loudness


def split_up(count, total, bound, lean):
    weights = [(1 << 20) // math.isqrt(rank ** lean) + 1 for rank in range(2, count + 1)]
    rest, counts = total - bound - (count - 1), [1] * (count - 1)
    while rest > 0:
        movable = [i for i in range(count - 1) if counts[i] < bound]
        whole, left = sum([weights[i] for i in movable]), rest
        for i in movable:
            more = min(bound - counts[i], max(1, left * weights[i] // whole), rest)
            counts[i] = counts[i] + more
            rest = rest - more
    return np.array([bound] + counts)


def uneven_parts(key, number_of, total, limit, slope):
    if number_of == 2:
        one = jax.random.randint(key, (), max(1, total - limit), min(limit, total - 1) + 1)
        return jnp.stack([one, total - one])
    tallies = jnp.asarray(split_up(number_of, total, limit, slope), jnp.int32)
    pairs = (number_of - 1) // 2
    giver, sink = tallies[1:1 + 2 * pairs:2], tallies[2:2 + 2 * pairs:2]
    room = jnp.minimum(giver - 1, limit - sink)
    moved = jax.random.randint(jax.random.fold_in(key, 1), (pairs,), 0, 1 << 20) % (room + 1)
    tallies = tallies.at[1:1 + 2 * pairs:2].set(giver - moved).at[2:2 + 2 * pairs:2].set(sink + moved)
    return tallies[jax.random.permutation(jax.random.fold_in(key, 2), number_of)]


def gaussian(rng, dims, spread, most, pieces=(), kind=jnp.bfloat16):
    gain = level_of(rng, dims, pieces, -0.22, 0.18) if pieces else 1.0
    values = jax.random.normal(rng, dims, jnp.float32) * spread * gain
    return jnp.minimum(jnp.maximum(values, -most), most).astype(kind)


def setup_inputs(seed: int = 0, part: int = 0) -> dict:
    key_of = jax.random.split(jax.random.key(seed), 7)
    part_keys = jax.random.split(jax.random.fold_in(key_of[6], part), 7)
    return {
        "tokens": gaussian(part_keys[0], (SEQ, D), 1.0, 6.0, ((0, 32), (1, 4))),
        "query": draw_query(jax.random.fold_in(jax.random.fold_in(key_of[6], part), 71), part),
        "w_key": gaussian(key_of[2], (D, KVH * HD), D ** -0.5, 0.09375, ((1, 4),)),
        "w_value": gaussian(key_of[3], (D, KVH * HD), D ** -0.5, 0.09375, ((1, 4),)),
        "doc_lengths": uneven_parts(part_keys[4], NDOCS, SEQ, L_MAX, 2).astype(jnp.int32),
        "balance": jax.vmap(lambda own: jax.random.permutation(own, N_CTX))(jax.random.split(part_keys[5], N_CTX)).reshape((N_CTX, N_CTX)).astype(jnp.int32),
    }


rope_base = 500000.0


def relaid_positions(balance):
    inverse = jnp.argsort(balance, axis=1).astype(jnp.int32)
    source = jnp.arange(N_CTX, dtype=jnp.int32)
    starts = source[None, :] * TOK_DEV + inverse.T * BROW
    return (starts[:, :, None] + jnp.arange(BROW, dtype=jnp.int32)[None, None, :]).reshape(-1)


def document_ids(positions, doc_lengths):
    bounds = jnp.cumsum(doc_lengths).astype(jnp.int32)
    return jnp.sum((positions[:, None] >= bounds[None, :]).astype(jnp.int32), axis=1)


def rotate(keys_raw, positions):
    half = HD // 2
    freq = rope_base ** (-(jnp.arange(half, dtype=jnp.float32) * 2.0 / HD))
    angle = positions.astype(jnp.float32)[:, None] * freq[None, :]
    cosine = jnp.cos(angle)[:, None, :]
    sine = jnp.sin(angle)[:, None, :]
    first = keys_raw[..., :half]
    second = keys_raw[..., half:]
    return jnp.concatenate([first * cosine - second * sine, second * cosine + first * sine], axis=-1)


def reference(tokens, query, w_key, w_value, doc_lengths, balance):
    positions = jnp.arange(SEQ, dtype=jnp.int32)
    docs = document_ids(positions, doc_lengths)
    keys_raw = jnp.dot(tokens, w_key, preferred_element_type=jnp.float32).reshape(SEQ, KVH, HD)
    keys = rotate(keys_raw, positions).astype(jnp.bfloat16)
    values = jnp.dot(tokens, w_value, preferred_element_type=jnp.float32).astype(jnp.bfloat16).reshape(SEQ, KVH, HD)
    order = relaid_positions(balance)
    group = QH // KVH
    qblock = 512
    nblocks = SEQ // qblock
    queries = jnp.take(query, order, axis=0).reshape(nblocks, qblock, KVH, group, HD)
    qpositions = order.reshape(nblocks, qblock)
    qdocs = jnp.take(docs, order, axis=0).reshape(nblocks, qblock)
    scale = 1.0 / (HD ** 0.5)

    def one_block(items):
        qrows, qpos, qdoc = items
        allowed = (positions[None, :] <= qpos[:, None]) & (docs[None, :] == qdoc[:, None])

        def one_head(index):
            qhead = lax.dynamic_index_in_dim(qrows, index, 1, keepdims=False).astype(jnp.float32)
            khead = lax.dynamic_index_in_dim(keys, index, 1, keepdims=False).astype(jnp.float32)
            vhead = lax.dynamic_index_in_dim(values, index, 1, keepdims=False).astype(jnp.float32)
            scores = jnp.einsum('qgd,kd->gqk', qhead, khead) * scale
            scores = jnp.where(allowed[None], scores, -1e30)
            top = jnp.max(scores, axis=-1, keepdims=True)
            weights = jnp.where(allowed[None], jnp.exp(scores - top), 0.0)
            total = jnp.sum(weights, axis=-1)
            rounded = lax.optimization_barrier(weights.astype(jnp.bfloat16)).astype(jnp.float32)
            summed = jnp.einsum('gqk,kd->qgd', rounded, vhead)
            return summed / total.T[:, :, None]

        heads = lax.map(one_head, jnp.arange(KVH, dtype=jnp.int32))
        return heads.transpose(1, 0, 2, 3).reshape(qblock, QH * HD)

    result = lax.map(one_block, (queries, qpositions, qdocs))
    return result.reshape(SEQ, QH * HD).astype(jnp.bfloat16)
```

```python
import functools

import jax
import jax.numpy as jnp
import numpy as np
from jax import lax
from jax.experimental import pallas as pl
from jax.experimental.pallas import tpu as pltpu
from jax.sharding import PartitionSpec as P

HD = 128
GROUP = 4
ROWS = 256
BROW = 8
NCTX = 32
NHEAD = 4
NDOCS = 16
FEAT = 1024
BEHIND = 8
ROPE_BASE = 500000.0
MASKED = -1e30
MESH = pl.DeviceIdType.MESH

SHIFT = 2
CHUNKS = 8
DEPTH = 3

R = ROWS // CHUNKS
BACKWARD = SHIFT
FORWARD = BEHIND // 2 - SHIFT
HOPS = max(FORWARD, BACKWARD)
LAG = 2 + (HOPS - 1) // 2
OWN = BEHIND - 2 * SHIFT
QROWS = GROUP * ROWS
RB = 128
BLOCK = GROUP * BROW
EXPC = float(np.log2(np.e) / np.sqrt(HD))

F32 = jnp.float32
BF16 = jnp.bfloat16


def when(cond):
    if isinstance(cond, (bool, np.bool_)):
        return (lambda f: f()) if cond else (lambda f: None)
    return pl.when(cond)


def both(*conds):
    out = True
    for c in conds:
        if isinstance(c, (bool, np.bool_)):
            if not c:
                return False
        else:
            out = c if out is True else jnp.logical_and(out, c)
    return out


def kernel(
    tokens, query, w_key, w_value, lengths, balance, freq, out,
    gath, wkv, part, cosf, sinf, kv, kvd, qbuf, q2, qidx, mx, tot, acc, stage, recv,
    local_sem, tsend, trecv, zsend, zrecv, ssend, srecv, qsend, qrecv, osend, orecv,
):
    x = lax.axis_index("dp")
    me = lax.axis_index("ctx")
    y = lax.axis_index("head")
    z = me // 2
    core = lax.rem(me, 2)
    up = lax.rem(y + 1, NHEAD)
    down = lax.rem(y + NHEAD - 1, NHEAD)
    opposite = lax.rem(y + 2, NHEAD)
    ahead = lax.rem(me + 2, NCTX)
    behind = lax.rem(me + NCTX - 2, NCTX)
    sibling = me + 1 - 2 * core
    qshard = lax.rem(me + 2 * SHIFT, NCTX)

    def remote(src, dst, ssem, rsem, ctx, head):
        return pltpu.make_async_remote_copy(
            src_ref=src, dst_ref=dst, send_sem=ssem, recv_sem=rsem,
            device_id=(x, ctx, head), device_id_type=MESH,
        )

    def own_copy(c, p):
        rows = pl.ds(c * R, R)
        return remote(
            tokens.at[rows, :], gath.at[1 + p, rows, :], tsend.at[p, c], trecv.at[p, c],
            me, up if p == 0 else down,
        )

    def relay_copy(c, p):
        rows = pl.ds(c * R + p * (R // 2), R // 2)
        return remote(
            gath.at[1 + p, rows, :], gath.at[3, rows, :], tsend.at[2 + p, c], trecv.at[2 + p, c],
            me, up if p == 0 else down,
        )

    def slot(c, u):
        if u == BEHIND:
            return kvd.at[pl.ds(c * R, R), pl.ds(0, 2 * HD)]
        return kv.at[c, pl.ds(u * R, R), pl.ds(0, 2 * HD)]

    def hop_copy(c, sign, h):
        index = h - 1 if sign > 0 else FORWARD + h - 1
        return remote(
            slot(c, OWN - sign * 2 * (h - 1)), slot(c, OWN - sign * 2 * h),
            zsend.at[index, c], zrecv.at[index, c], ahead if sign > 0 else behind, y,
        )

    def sib_copy(c, u):
        there = pl.multiple_of((u - 1 + 2 * core) * R, R)
        return remote(
            slot(c, u), kv.at[c, pl.ds(there, R), pl.ds(0, 2 * HD)],
            ssend.at[u // 2, c], srecv.at[u // 2 - 1 + core, c], sibling, y,
        )

    def sib_cond(u):
        if u == 0:
            return core == 1
        if u == BEHIND:
            return core == 0
        return True

    def sib_start(c, u):
        @when(sib_cond(u))
        def _():
            sib_copy(c, u).start()

    def sib_wait(c, k):
        remote(
            slot(c, 2 * k), slot(c, 2 * k + 1), ssend.at[k, c], srecv.at[k, c], sibling, y
        ).wait_recv()

    query_copy = remote(
        query, qbuf, qsend.at[0], qrecv.at[0], lax.rem(me + NCTX - 2 * SHIFT, NCTX), y
    )

    barrier = pltpu.get_barrier_semaphore()

    def greet(o, carry):
        pl.semaphore_signal(
            barrier, inc=1, device_id=(x, lax.rem(me + o, NCTX), y), device_id_type=MESH
        )
        return carry

    for head in (up, down):
        pl.semaphore_signal(barrier, inc=1, device_id=(x, me, head), device_id_type=MESH)
    lax.fori_loop(1, NCTX, greet, 0)

    loads = [
        pltpu.make_async_copy(tokens, gath.at[0], local_sem.at[0]),
        pltpu.make_async_copy(w_value, wkv.at[:, pl.ds(0, HD)], local_sem.at[1]),
        pltpu.make_async_copy(w_key, wkv.at[:, pl.ds(HD, HD)], local_sem.at[2]),
    ]
    if SHIFT == 0:
        loads.append(pltpu.make_async_copy(query, qbuf, local_sem.at[3]))
    for load in loads:
        load.start()

    pl.semaphore_wait(barrier, NCTX - 1 + 2)

    for c in range(DEPTH):
        for p in range(2):
            own_copy(c, p).start()
    if SHIFT:
        query_copy.start()

    lane = lax.broadcasted_iota(jnp.int32, (1, HD), 1)
    low = jnp.zeros((1, HD), jnp.int32)
    high = jnp.zeros((1, HD), jnp.int32)
    edge = jnp.int32(0)
    for j in range(NDOCS):
        low = jnp.where(lane == j, edge, low)
        edge = edge + lengths[j]
        high = jnp.where(lane == j, edge, high)

    def in_doc(pos):
        return (pos >= low) & (pos < high)

    pos = me * ROWS + lax.broadcasted_iota(jnp.int32, (ROWS, HD), 0)
    angle = pos.astype(F32) * freq[...]
    cosf[...] = jnp.cos(angle)
    sine = jnp.sin(angle)
    sinf[...] = jnp.where(lax.broadcasted_iota(jnp.int32, (ROWS, HD), 1) < HD // 2, -sine, sine)

    def mark(c, carry):
        row = lax.broadcasted_iota(jnp.int32, (BEHIND * R, HD), 0)
        shard = (me + NCTX - BEHIND + 2 * SHIFT + row // R) & (NCTX - 1)
        kpos = shard * ROWS + c * R + (row & (R - 1))
        kv[c, :, pl.ds(2 * HD, HD)] = jnp.where(in_doc(kpos), 0.0, MASKED).astype(BF16)
        return carry

    lax.fori_loop(0, CHUNKS, mark, 0)
    qpos = qshard * ROWS + lax.broadcasted_iota(jnp.int32, (ROWS, HD), 0)
    kvd[:, pl.ds(2 * HD, HD)] = jnp.where(in_doc(qpos), 0.0, MASKED).astype(BF16)

    mx[...] = jnp.full_like(mx, MASKED)
    tot[...] = jnp.zeros_like(tot)
    acc[...] = jnp.zeros_like(acc)
    for load in loads:
        load.wait()

    def dest_of(n, e):
        if isinstance(n, int):
            dz = 8 - n if e < 2 else (0 if n == 0 else n - 8)
        else:
            dz = 8 - n if e < 2 else jnp.where(n == 0, 0, n - 8)
        return ((z + 16 + dz) & 15) * 2 + ((core + e) & 1)

    def prepare_query():
        if SHIFT:
            query_copy.wait_recv()
        r = lax.broadcasted_iota(jnp.int32, (ROWS, NCTX), 0)
        n = r >> 5
        e = (r >> 3) & 3
        dz = jnp.where(e < 2, 8 - n, jnp.where(n == 0, 0, n - 8))
        dest = ((z + 16 + dz) & 15) * 2 + ((core + e) & 1)
        bal = balance[pl.ds(qshard, 1), :]
        pick = jnp.where(bal == dest, 1.0, 0.0).astype(BF16)
        b = lax.broadcasted_iota(jnp.int32, (NCTX, ROWS), 0)
        c = lax.broadcasted_iota(jnp.int32, (NCTX, ROWS), 1)
        widen = jnp.where((c >> 3) == b, 1.0, 0.0).astype(BF16)
        spread = jnp.dot(pick, widen, preferred_element_type=F32)
        r = lax.broadcasted_iota(jnp.int32, (ROWS, ROWS), 0)
        c = lax.broadcasted_iota(jnp.int32, (ROWS, ROWS), 1)
        perm = jnp.where((c & 7) == (r & 7), spread, 0.0).astype(BF16)
        moved = jnp.dot(perm, qbuf[...], preferred_element_type=F32)
        doc = jnp.where(in_doc(qpos), 1.0, 0.0).astype(BF16)
        doc = jnp.dot(perm, doc, preferred_element_type=F32)
        index = lax.broadcasted_iota(jnp.int32, (ROWS, HD), 0).astype(F32).astype(BF16)
        index = jnp.dot(perm, index, preferred_element_type=F32)

        def rows_of(parts):
            parts = [p.reshape(NCTX, BROW, HD) for p in parts]
            return jnp.stack(parts, axis=1).reshape(QROWS, HD)

        q2[:, pl.ds(0, HD)] = rows_of(
            [moved[:, g * HD : (g + 1) * HD] for g in range(GROUP)]
        ).astype(BF16)
        q2[:, pl.ds(HD, HD)] = rows_of([doc] * GROUP).astype(BF16)
        qidx[...] = rows_of([index] * GROUP)

    def nt(a, b):
        return lax.dot_general(a, b, (((1,), (1,)), ((), ())), preferred_element_type=F32)

    def update(rows, score, values):
        width = score.shape[1]
        old = mx[rows, :]
        new = jnp.maximum(old, jnp.max(score, axis=1, keepdims=True))
        keep = jnp.exp2((old - new) * EXPC)
        wide = jnp.concatenate([new] * (width // HD), axis=1) if width > HD else new
        weight = jnp.exp2((score - wide) * EXPC)
        lanes = weight[:, :HD]
        for k in range(1, width // HD):
            lanes = lanes + weight[:, k * HD : (k + 1) * HD]
        mx[rows, :] = new
        tot[rows, :] = tot[rows, :] * keep + lanes
        acc[rows, :] = acc[rows, :] * keep + jnp.dot(
            weight.astype(BF16), values, preferred_element_type=F32
        )

    def plain(c, rows):
        score = nt(q2[rows, :], kv[c, :, pl.ds(HD, 2 * HD)])
        update(rows, score, kv[c, :, pl.ds(0, HD)])

    def diagonal(half, rows):
        keys = pl.ds(half * HD, HD)
        score = nt(q2[rows, :], kvd[keys, pl.ds(HD, 2 * HD)])
        kidx = (half * HD + lax.broadcasted_iota(jnp.int32, (RB, HD), 1)).astype(F32)
        score = jnp.where(kidx <= qidx[rows, :], score, MASKED)
        update(rows, score, kvd[keys, pl.ds(0, HD)])

    def out_copy(n, e):
        rows = pl.ds(pl.multiple_of((n * 4 + e) * BLOCK, BLOCK), BLOCK)
        there = pl.ds(pl.multiple_of(qshard * BLOCK, BLOCK), BLOCK)
        return remote(
            stage.at[rows, :], recv.at[there, :], osend.at[n * 4 + e], orecv.at[qshard],
            dest_of(n, e), y,
        )

    def hops(c, h):
        if h <= FORWARD:
            hop_copy(c, 1, h).wait_recv()
            if h < FORWARD:
                hop_copy(c, 1, h + 1).start()
            sib_start(c, OWN - 2 * h)
        if h <= BACKWARD:
            hop_copy(c, -1, h).wait_recv()
            if h < BACKWARD:
                hop_copy(c, -1, h + 1).start()
            sib_start(c, OWN + 2 * h)

    def iteration(i, last):
        @when(i < CHUNKS)
        def _():
            for p in range(2):
                own_copy(i, p).wait_recv()
                relay_copy(i, p).start()

        @when(i + DEPTH < CHUNKS)
        def _():
            for p in range(2):
                own_copy(i + DEPTH, p).start()

        for h in range(1, HOPS + 1, 2):
            c = i - 2 - h // 2

            @when(both(c >= 0, c < CHUNKS))
            def _():
                hops(c, h)

        @when(i < CHUNKS)
        def _():
            rows = pl.ds(i * R, R)
            total = None
            for s, source in enumerate((y, down, up)):
                term = jnp.dot(
                    gath[s, rows, :], wkv[pl.ds(pl.multiple_of(source * FEAT, FEAT), FEAT), :],
                    preferred_element_type=F32,
                )
                total = term if total is None else total + term
            part[rows, :] = total

        @when(both(i >= 1, i <= CHUNKS))
        def _():
            c = i - 1
            rows = pl.ds(c * R, R)
            for p in range(2):
                relay_copy(c, p).wait_recv()
            raw = part[rows, :] + jnp.dot(
                gath[3, rows, :], wkv[pl.ds(pl.multiple_of(opposite * FEAT, FEAT), FEAT), :],
                preferred_element_type=F32,
            )
            value = raw[:, :HD]
            key = raw[:, HD:]
            key = key * cosf[rows, :] + pltpu.roll(key, HD // 2, 1) * sinf[rows, :]
            slot(c, OWN)[...] = jnp.concatenate([value, key], axis=1).astype(BF16)
            if FORWARD:
                hop_copy(c, 1, 1).start()
            if BACKWARD:
                hop_copy(c, -1, 1).start()
            sib_start(c, OWN)

        for h in range(2, HOPS + 1, 2):
            c = i - 2 - (h - 1) // 2

            @when(both(c >= 0, c < CHUNKS))
            def _():
                hops(c, h)

        a = i - LAG
        if last:
            for k in range(4):
                sib_wait(a, k)
        else:
            @when(i == LAG)
            def _():
                prepare_query()

            @when(a >= 0)
            def _():
                for k in range(4):
                    sib_wait(a, k)

                def block(rb, carry):
                    plain(a, pl.ds(pl.multiple_of(rb * RB, RB), RB))
                    return carry

                lax.fori_loop(0, QROWS // RB, block, 0)

            @when(a == CHUNKS // 2 - 1)
            def _():
                def block(rb, carry):
                    diagonal(0, pl.ds(pl.multiple_of(rb * RB, RB), RB))
                    return carry

                lax.fori_loop(0, QROWS // RB, block, 0)

    def loop_body(i, carry):
        iteration(i, False)
        return carry

    final = CHUNKS + LAG - 1
    lax.fori_loop(0, final, loop_body, 0)
    iteration(final, True)

    def finish(rb, carry):
        rows = pl.ds(pl.multiple_of(rb * RB, RB), RB)
        plain(CHUNKS - 1, rows)
        diagonal(1, rows)
        total = jnp.sum(tot[rows, :], axis=1, keepdims=True)
        stage[rows, :] = (acc[rows, :] / total).astype(BF16)
        for e in range(4):
            if e == 2:
                @pl.when(rb > 0)
                def _():
                    out_copy(rb, e).start()
            else:
                out_copy(rb, e).start()
        return carry

    lax.fori_loop(0, QROWS // RB, finish, 0)

    def arrive(dz, own):
        source = (z + 16 + dz) & 15
        chip = (source + SHIFT) & 15
        for k in range(2):
            shard = chip * 2 + k
            there = pl.ds(pl.multiple_of(shard * BLOCK, BLOCK), BLOCK)

            def landed():
                remote(
                    stage.at[pl.ds(0, BLOCK), :], recv.at[there, :], osend.at[0], orecv.at[shard],
                    sibling, y,
                ).wait_recv()

            if own:
                pl.when(core != k)(landed)
            else:
                landed()
        if own:
            there = pl.ds(pl.multiple_of(qshard * BLOCK, BLOCK), BLOCK)
            recv[there, :] = stage[pl.ds(2 * BLOCK, BLOCK), :]
        block = recv[pl.ds(pl.multiple_of(chip * 2 * BLOCK, 2 * BLOCK), 2 * BLOCK), :].astype(F32)
        heads = [
            jnp.concatenate(
                [
                    block[g * BROW : (g + 1) * BROW],
                    block[BLOCK + g * BROW : BLOCK + (g + 1) * BROW],
                ],
                axis=0,
            )
            for g in range(GROUP)
        ]
        out[pl.ds(pl.multiple_of(chip * 2 * BROW, 2 * BROW), 2 * BROW), :] = jnp.concatenate(
            heads, axis=1
        ).astype(BF16)

    arrive(0, True)
    arrive(8, False)

    def pair(n, carry):
        arrive(8 - n, False)
        arrive(n - 8, False)
        return carry

    lax.fori_loop(1, 8, pair, 0)

    def sent(c, carry):
        for p in range(2):
            own_copy(c, p).wait_send()
            relay_copy(c, p).wait_send()
        for h in range(1, FORWARD + 1):
            hop_copy(c, 1, h).wait_send()
        for h in range(1, BACKWARD + 1):
            hop_copy(c, -1, h).wait_send()
        for u in range(0, BEHIND + 1, 2):
            @when(sib_cond(u))
            def _():
                sib_copy(c, u).wait_send()
        return carry

    lax.fori_loop(0, CHUNKS, sent, 0)
    if SHIFT:
        query_copy.wait_send()

    def out_sent(n, carry):
        for e in range(4):
            if e == 2:
                @pl.when(n > 0)
                def _():
                    out_copy(n, e).wait_send()
            else:
                out_copy(n, e).wait_send()
        return carry

    lax.fori_loop(0, QROWS // RB, out_sent, 0)


def local(tokens, query, w_key, w_value, doc_lengths, balance):
    half = HD // 2
    freq = ROPE_BASE ** (-(jnp.arange(half, dtype=F32) * 2.0 / HD))
    freq = jnp.concatenate([freq, freq])[None, :]
    anywhere = pl.BlockSpec(memory_space=pl.ANY)
    vmem = pl.BlockSpec(memory_space=pltpu.VMEM)
    smem = pl.BlockSpec(memory_space=pltpu.SMEM)
    dma = pltpu.SemaphoreType.DMA
    width = 2 * HD
    return pl.pallas_call(
        kernel,
        out_shape=jax.ShapeDtypeStruct((ROWS, GROUP * HD), BF16),
        in_specs=[anywhere, anywhere, anywhere, anywhere, smem, vmem, vmem],
        out_specs=vmem,
        scratch_shapes=[
            pltpu.VMEM((NHEAD, ROWS, FEAT), BF16),
            pltpu.VMEM((NHEAD * FEAT, width), BF16),
            pltpu.VMEM((ROWS, width), F32),
            pltpu.VMEM((ROWS, HD), F32),
            pltpu.VMEM((ROWS, HD), F32),
            pltpu.VMEM((CHUNKS, BEHIND * R, 3 * HD), BF16),
            pltpu.VMEM((ROWS, 3 * HD), BF16),
            pltpu.VMEM((ROWS, GROUP * HD), BF16),
            pltpu.VMEM((QROWS, width), BF16),
            pltpu.VMEM((QROWS, HD), F32),
            pltpu.VMEM((QROWS, HD), F32),
            pltpu.VMEM((QROWS, HD), F32),
            pltpu.VMEM((QROWS, HD), F32),
            pltpu.VMEM((QROWS, HD), BF16),
            pltpu.VMEM((QROWS, HD), BF16),
            dma((4,)),
            dma((4, CHUNKS)),
            dma((4, CHUNKS)),
            dma((FORWARD + BACKWARD, CHUNKS)),
            dma((FORWARD + BACKWARD, CHUNKS)),
            dma((5, CHUNKS)),
            dma((4, CHUNKS)),
            dma((1,)),
            dma((1,)),
            dma((NCTX,)),
            dma((NCTX,)),
        ],
        compiler_params=pltpu.CompilerParams(
            collective_id=0, has_side_effects=True, vmem_limit_bytes=48 * 1024 * 1024
        ),
        name="attend",
    )(tokens, query, w_key, w_value, doc_lengths, balance, freq)


def solution(mesh):
    placed = (
        P(("dp", "ctx"), "head"),
        P(("dp", "ctx"), "head"),
        P(None, "head"),
        P(None, "head"),
        P("dp"),
        P("dp", None),
    )
    return jax.shard_map(
        local, mesh=mesh, in_specs=placed, out_specs=P(("dp", "ctx"), "head"), check_vma=False
    )
```

```python
import functools

import jax
import jax.numpy as jnp
import numpy as np
from jax import lax
from jax.experimental import pallas as pl
from jax.experimental.pallas import tpu as pltpu
from jax.sharding import PartitionSpec as P

HD = 128
GROUP = 4
ROWS = 256
BROW = 8
NCTX = 32
NHEAD = 4
NDOCS = 16
FEAT = 1024
BEHIND = 8
ROPE_BASE = 500000.0
MASKED = -1e30
MESH = pl.DeviceIdType.MESH

SHIFT = 2
CHUNKS = 8
DEPTH = 3
LAG_OPP = 3
LAG_HOP = 5

R = ROWS // CHUNKS
BACKWARD = SHIFT
FORWARD = BEHIND // 2 - SHIFT
GROUPS = CHUNKS // 2
OWN = BEHIND - 2 * SHIFT
QROWS = GROUP * ROWS
KEYS = 2 * BEHIND * R
BLOCK = GROUP * BROW
ROUNDS = NCTX // 4 - 1
EXPC = float(np.log2(np.e) / np.sqrt(HD))

F32 = jnp.float32
BF16 = jnp.bfloat16


def when(cond):
    if isinstance(cond, (bool, np.bool_)):
        return (lambda f: f()) if cond else (lambda f: None)
    return pl.when(cond)


def both(*conds):
    out = True
    for c in conds:
        if isinstance(c, (bool, np.bool_)):
            if not c:
                return False
        else:
            out = c if out is True else jnp.logical_and(out, c)
    return out


def kernel(
    tokens, query, w_key, w_value, lengths, balance, freq, out,
    gath, wkv, part, cosf, sinf, kv, kvd, qbuf, q2, qidx, mx, tot, acc, stage, recv,
    local_sem, tsend, trecv, zsend, zrecv, srecv, qsend, qrecv, osend, orecv, round_sem,
):
    x = lax.axis_index("dp")
    me = lax.axis_index("ctx")
    y = lax.axis_index("head")
    z = me // 2
    core = lax.rem(me, 2)
    up = lax.rem(y + 1, NHEAD)
    down = lax.rem(y + NHEAD - 1, NHEAD)
    opposite = lax.rem(y + 2, NHEAD)
    sibling = me + 1 - 2 * core
    qshard = lax.rem(me + 2 * SHIFT, NCTX)

    def remote(src, dst, ssem, rsem, ctx, head):
        return pltpu.make_async_remote_copy(
            src_ref=src, dst_ref=dst, send_sem=ssem, recv_sem=rsem,
            device_id=(x, ctx, head), device_id_type=MESH,
        )

    def own_copy(c, p):
        rows = pl.ds(c * R, R)
        return remote(
            tokens.at[rows, :], gath.at[1 + p, rows, :], tsend.at[0], trecv.at[p, c],
            me, up if p == 0 else down,
        )

    def relay_copy(c, p):
        rows = pl.ds(c * R + p * (R // 2), R // 2)
        return remote(
            gath.at[1 + p, rows, :], gath.at[3, rows, :], tsend.at[0], trecv.at[2 + p, c],
            me, up if p == 0 else down,
        )

    def slot(c, u):
        if u == BEHIND:
            return kvd.at[pl.ds(c * R, R), pl.ds(0, 2 * HD)]
        return kv.at[c // 2, pl.ds(lax.rem(c, 2) * (BEHIND * R) + u * R, R), pl.ds(0, 2 * HD)]

    def hop_copy(c, sign, h):
        index = h - 1 if sign > 0 else FORWARD + h - 1
        return remote(
            slot(c, OWN), slot(c, OWN - sign * 2 * h), zsend.at[0], zrecv.at[index, c],
            lax.rem(me + NCTX + sign * 2 * h, NCTX), y,
        )

    def sib_copy(c, u):
        there = pl.multiple_of(lax.rem(c, 2) * (BEHIND * R) + (u - 1 + 2 * core) * R, R)
        return remote(
            slot(c, u), kv.at[c // 2, pl.ds(there, R), pl.ds(0, 2 * HD)],
            zsend.at[0], srecv.at[u // 2 - 1 + core, c], sibling, y,
        )

    def sib_cond(u):
        if u == 0:
            return core == 1
        if u == BEHIND:
            return core == 0
        return True

    def sib_start(c, u):
        @when(sib_cond(u))
        def _():
            sib_copy(c, u).start()

    def sib_wait(c, k):
        remote(
            slot(c, 2 * k), slot(c, 2 * k + 1), zsend.at[0], srecv.at[k, c], sibling, y
        ).wait_recv()

    query_copy = remote(
        query, qbuf, qsend.at[0], qrecv.at[0], lax.rem(me + NCTX - 2 * SHIFT, NCTX), y
    )

    barrier = pltpu.get_barrier_semaphore()

    ahead = lax.rem(me + 2, NCTX)
    astern = lax.rem(me + NCTX - 2, NCTX)
    for ctx, head in ((me, up), (me, down), (ahead, y), (astern, y), (sibling, y)):
        pl.semaphore_signal(barrier, inc=1, device_id=(x, ctx, head), device_id_type=MESH)

    def tell(k):
        for ctx in (ahead, astern):
            pl.semaphore_signal(
                round_sem.at[k], inc=1, device_id=(x, ctx, y), device_id_type=MESH
            )

    loads = [
        pltpu.make_async_copy(tokens, gath.at[0], local_sem.at[0]),
        pltpu.make_async_copy(w_value, wkv.at[:, pl.ds(0, HD)], local_sem.at[1]),
        pltpu.make_async_copy(w_key, wkv.at[:, pl.ds(HD, HD)], local_sem.at[2]),
    ]
    if SHIFT == 0:
        loads.append(pltpu.make_async_copy(query, qbuf, local_sem.at[3]))
    for load in loads:
        load.start()

    pl.semaphore_wait(barrier, 5)

    for c in range(DEPTH):
        for p in range(2):
            own_copy(c, p).start()
    tell(0)

    lane = lax.broadcasted_iota(jnp.int32, (1, HD), 1)
    low = jnp.zeros((1, HD), jnp.int32)
    high = jnp.zeros((1, HD), jnp.int32)
    edge = jnp.int32(0)
    for j in range(NDOCS):
        low = jnp.where(lane == j, edge, low)
        edge = edge + lengths[j]
        high = jnp.where(lane == j, edge, high)

    def in_doc(pos):
        return (pos >= low) & (pos < high)

    pos = me * ROWS + lax.broadcasted_iota(jnp.int32, (ROWS, HD), 0)
    angle = pos.astype(F32) * freq[...]
    cosf[...] = jnp.cos(angle)
    sine = jnp.sin(angle)
    sinf[...] = jnp.where(lax.broadcasted_iota(jnp.int32, (ROWS, HD), 1) < HD // 2, -sine, sine)

    def mark(c, carry):
        row = lax.broadcasted_iota(jnp.int32, (BEHIND * R, HD), 0)
        shard = (me + NCTX - BEHIND + 2 * SHIFT + row // R) & (NCTX - 1)
        kpos = shard * ROWS + c * R + (row & (R - 1))
        half = pl.ds(pl.multiple_of(lax.rem(c, 2) * (BEHIND * R), BEHIND * R), BEHIND * R)
        kv[c // 2, half, pl.ds(2 * HD, HD)] = jnp.where(in_doc(kpos), 0.0, MASKED).astype(BF16)
        return carry

    lax.fori_loop(0, CHUNKS, mark, 0)
    qpos = qshard * ROWS + lax.broadcasted_iota(jnp.int32, (ROWS, HD), 0)
    kvd[:, pl.ds(2 * HD, HD)] = jnp.where(in_doc(qpos), 0.0, MASKED).astype(BF16)

    mx[...] = jnp.full_like(mx, MASKED)
    tot[...] = jnp.zeros_like(tot)
    acc[...] = jnp.zeros_like(acc)
    for load in loads:
        load.wait()

    def dest_of(n, e):
        if isinstance(n, int):
            dz = 8 - n if e < 2 else (0 if n == 0 else n - 8)
        else:
            dz = 8 - n if e < 2 else jnp.where(n == 0, 0, n - 8)
        return ((z + 16 + dz) & 15) * 2 + ((core + e) & 1)

    def prepare_query():
        if SHIFT:
            query_copy.wait_recv()
        r = lax.broadcasted_iota(jnp.int32, (ROWS, NCTX), 0)
        n = r >> 5
        e = (r >> 3) & 3
        dz = jnp.where(e < 2, 8 - n, jnp.where(n == 0, 0, n - 8))
        dest = ((z + 16 + dz) & 15) * 2 + ((core + e) & 1)
        bal = balance[pl.ds(qshard, 1), :]
        pick = jnp.where(bal == dest, 1.0, 0.0).astype(BF16)
        b = lax.broadcasted_iota(jnp.int32, (NCTX, ROWS), 0)
        c = lax.broadcasted_iota(jnp.int32, (NCTX, ROWS), 1)
        widen = jnp.where((c >> 3) == b, 1.0, 0.0).astype(BF16)
        spread = jnp.dot(pick, widen, preferred_element_type=F32)
        r = lax.broadcasted_iota(jnp.int32, (ROWS, ROWS), 0)
        c = lax.broadcasted_iota(jnp.int32, (ROWS, ROWS), 1)
        perm = jnp.where((c & 7) == (r & 7), spread, 0.0).astype(BF16)
        moved = jnp.dot(perm, qbuf[...], preferred_element_type=F32)
        doc = jnp.where(in_doc(qpos), 1.0, 0.0).astype(BF16)
        doc = jnp.dot(perm, doc, preferred_element_type=F32)
        index = lax.broadcasted_iota(jnp.int32, (ROWS, HD), 0).astype(F32).astype(BF16)
        index = jnp.dot(perm, index, preferred_element_type=F32)

        def rows_of(parts):
            parts = [p.reshape(NCTX, BROW, HD) for p in parts]
            return jnp.stack(parts, axis=1).reshape(QROWS, HD)

        q2[:, pl.ds(0, HD)] = rows_of(
            [moved[:, g * HD : (g + 1) * HD] for g in range(GROUP)]
        ).astype(BF16)
        q2[:, pl.ds(HD, HD)] = rows_of([doc] * GROUP).astype(BF16)
        qidx[...] = rows_of([index] * GROUP)

    def nt(a, b):
        return lax.dot_general(a, b, (((1,), (1,)), ((), ())), preferred_element_type=F32)

    def update(score, values):
        width = score.shape[1]
        old = mx[...]
        new = jnp.maximum(old, jnp.max(score, axis=1, keepdims=True))
        keep = jnp.exp2((old - new) * EXPC)
        wide = jnp.concatenate([new] * (width // HD), axis=1) if width > HD else new
        weight = jnp.exp2((score - wide) * EXPC)
        lanes = weight[:, :HD]
        for k in range(1, width // HD):
            lanes = lanes + weight[:, k * HD : (k + 1) * HD]
        mx[...] = new
        tot[...] = tot[...] * keep + lanes
        acc[...] = acc[...] * keep + jnp.dot(
            weight.astype(BF16), values, preferred_element_type=F32
        )

    def plain(g):
        update(nt(q2[...], kv[g, :, pl.ds(HD, 2 * HD)]), kv[g, :, pl.ds(0, HD)])

    def diagonal(half):
        keys = pl.ds(pl.multiple_of(half * HD, HD), HD)
        score = nt(q2[...], kvd[keys, pl.ds(HD, 2 * HD)])
        kidx = (half * HD + lax.broadcasted_iota(jnp.int32, (QROWS, HD), 1)).astype(F32)
        update(jnp.where(kidx <= qidx[...], score, MASKED), kvd[keys, pl.ds(0, HD)])

    def out_copy(n, e):
        rows = pl.ds(pl.multiple_of((n * 4 + e) * BLOCK, BLOCK), BLOCK)
        there = pl.ds(pl.multiple_of(qshard * BLOCK, BLOCK), BLOCK)
        return remote(
            stage.at[rows, :], recv.at[there, :], osend.at[0], orecv.at[qshard],
            dest_of(n, e), y,
        )

    def hops(c):
        for sign, count in ((1, FORWARD), (-1, BACKWARD)):
            for h in range(1, count + 1):
                hop_copy(c, sign, h).wait_recv()
                sib_start(c, OWN - sign * 2 * h)

    def sib_arrived(g):
        for c in (2 * g, 2 * g + 1):
            for k in range(4):
                sib_wait(c, k)

    def finish(c):
        rows = pl.ds(c * R, R)
        for p in range(2):
            relay_copy(c, p).wait_recv()
        raw = part[rows, :] + jnp.dot(
            gath[3, rows, :], wkv[pl.ds(pl.multiple_of(opposite * FEAT, FEAT), FEAT), :],
            preferred_element_type=F32,
        )
        value = raw[:, :HD]
        key = raw[:, HD:]
        key = key * cosf[rows, :] + pltpu.roll(key, HD // 2, 1) * sinf[rows, :]
        slot(c, OWN)[...] = jnp.concatenate([value, key], axis=1).astype(BF16)
        for sign, count in ((1, FORWARD), (-1, BACKWARD)):
            for h in range(1, count + 1):
                hop_copy(c, sign, h).start()
        sib_start(c, OWN)

    def gather(i, carry):
        for p in range(2):
            own_copy(i, p).wait_recv()
            relay_copy(i, p).start()

        @pl.when(i + DEPTH < CHUNKS)
        def _():
            for p in range(2):
                own_copy(i + DEPTH, p).start()

        rows = pl.ds(i * R, R)
        total = None
        for s, source in enumerate((y, down, up)):
            term = jnp.dot(
                gath[s, rows, :], wkv[pl.ds(pl.multiple_of(source * FEAT, FEAT), FEAT), :],
                preferred_element_type=F32,
            )
            total = term if total is None else total + term
        part[rows, :] = total

        @pl.when(i >= LAG_OPP)
        def _():
            finish(i - LAG_OPP)

        @pl.when(i >= LAG_HOP)
        def _():
            hops(i - LAG_HOP)

        @pl.when(i < ROUNDS)
        def _():
            pl.semaphore_wait(round_sem.at[i], 2)

        @pl.when(i < ROUNDS - 1)
        def _():
            tell(i + 1)

        if SHIFT:
            @pl.when(i == 0)
            def _():
                query_copy.start()

        @pl.when(i == ROUNDS)
        def _():
            pl.semaphore_signal(
                round_sem.at[ROUNDS], inc=1, device_id=(x, sibling, y), device_id_type=MESH
            )
            pl.semaphore_wait(round_sem.at[ROUNDS], 1)

        return carry

    lax.fori_loop(0, CHUNKS, gather, 0)
    prepare_query()

    def finish_loop(c, carry):
        finish(c)
        return carry

    def hops_loop(c, carry):
        hops(c)
        return carry

    lax.fori_loop(CHUNKS - LAG_OPP, CHUNKS, finish_loop, 0)
    lax.fori_loop(CHUNKS - LAG_HOP, CHUNKS - 3, hops_loop, 0)

    def attend(g, carry):
        sib_arrived(g)
        plain(g)

        @pl.when(lax.rem(g, 2) == 1)
        def _():
            diagonal(g // 2)

        @pl.when(g < GROUPS - 1)
        def _():
            hops(g + CHUNKS - 3)

        return carry

    lax.fori_loop(0, GROUPS, attend, 0)

    total = jnp.sum(tot[...], axis=1, keepdims=True)
    stage[...] = (acc[...] / total).astype(BF16)

    def send(rb, carry):
        for e in range(4):
            if e == 2:
                @pl.when(rb > 0)
                def _():
                    out_copy(rb, e).start()
            else:
                out_copy(rb, e).start()
        return carry

    lax.fori_loop(0, QROWS // (4 * BLOCK), send, 0)

    def sent(block, sem):
        pltpu.make_async_copy(block, block, sem).wait()

    sent(gath.at[pl.ds(0, 3)], tsend.at[0])
    sent(gath.at[pl.ds(0, 2)], zsend.at[0])
    if SHIFT:
        query_copy.wait_send()

    def arrive(dz, own):
        source = (z + 16 + dz) & 15
        chip = (source + SHIFT) & 15
        for k in range(2):
            shard = chip * 2 + k
            there = pl.ds(pl.multiple_of(shard * BLOCK, BLOCK), BLOCK)

            def landed():
                remote(
                    stage.at[pl.ds(0, BLOCK), :], recv.at[there, :], osend.at[0], orecv.at[shard],
                    sibling, y,
                ).wait_recv()

            if own:
                pl.when(core != k)(landed)
            else:
                landed()
        if own:
            there = pl.ds(pl.multiple_of(qshard * BLOCK, BLOCK), BLOCK)
            recv[there, :] = stage[pl.ds(2 * BLOCK, BLOCK), :]
        block = recv[pl.ds(pl.multiple_of(chip * 2 * BLOCK, 2 * BLOCK), 2 * BLOCK), :].astype(F32)
        heads = [
            jnp.concatenate(
                [
                    block[g * BROW : (g + 1) * BROW],
                    block[BLOCK + g * BROW : BLOCK + (g + 1) * BROW],
                ],
                axis=0,
            )
            for g in range(GROUP)
        ]
        out[pl.ds(pl.multiple_of(chip * 2 * BROW, 2 * BROW), 2 * BROW), :] = jnp.concatenate(
            heads, axis=1
        ).astype(BF16)

    arrive(0, True)
    arrive(8, False)

    def pair(n, carry):
        arrive(8 - n, False)
        arrive(n - 8, False)
        return carry

    lax.fori_loop(1, 8, pair, 0)

    sent(stage.at[pl.ds(0, QROWS - BLOCK), :], osend.at[0])


def local(tokens, query, w_key, w_value, doc_lengths, balance):
    half = HD // 2
    freq = ROPE_BASE ** (-(jnp.arange(half, dtype=F32) * 2.0 / HD))
    freq = jnp.concatenate([freq, freq])[None, :]
    hbm = pl.BlockSpec(memory_space=pltpu.HBM)
    vmem = pl.BlockSpec(memory_space=pltpu.VMEM)
    smem = pl.BlockSpec(memory_space=pltpu.SMEM)
    dma = pltpu.SemaphoreType.DMA
    width = 2 * HD
    return pl.pallas_call(
        kernel,
        out_shape=jax.ShapeDtypeStruct((ROWS, GROUP * HD), BF16),
        in_specs=[hbm, hbm, hbm, hbm, smem, vmem, vmem],
        out_specs=vmem,
        scratch_shapes=[
            pltpu.VMEM((NHEAD, ROWS, FEAT), BF16),
            pltpu.VMEM((NHEAD * FEAT, width), BF16),
            pltpu.VMEM((ROWS, width), F32),
            pltpu.VMEM((ROWS, HD), F32),
            pltpu.VMEM((ROWS, HD), F32),
            pltpu.VMEM((GROUPS, KEYS, 3 * HD), BF16),
            pltpu.VMEM((ROWS, 3 * HD), BF16),
            pltpu.VMEM((ROWS, GROUP * HD), BF16),
            pltpu.VMEM((QROWS, width), BF16),
            pltpu.VMEM((QROWS, HD), F32),
            pltpu.VMEM((QROWS, HD), F32),
            pltpu.VMEM((QROWS, HD), F32),
            pltpu.VMEM((QROWS, HD), F32),
            pltpu.VMEM((QROWS, HD), BF16),
            pltpu.VMEM((QROWS, HD), BF16),
            dma((4,)),
            dma((1,)),
            dma((4, CHUNKS)),
            dma((1,)),
            dma((FORWARD + BACKWARD, CHUNKS)),
            dma((4, CHUNKS)),
            dma((1,)),
            dma((1,)),
            dma((1,)),
            dma((NCTX,)),
            pltpu.SemaphoreType.REGULAR((ROUNDS + 1,)),
        ],
        compiler_params=pltpu.CompilerParams(
            collective_id=0, has_side_effects=True, vmem_limit_bytes=60 * 1024 * 1024
        ),
        name="attend",
    )(tokens, query, w_key, w_value, doc_lengths, balance, freq)


def solution(mesh):
    placed = (
        P(("dp", "ctx"), "head"),
        P(("dp", "ctx"), "head"),
        P(None, "head"),
        P(None, "head"),
        P("dp"),
        P("dp", None),
    )
    return jax.shard_map(
        local, mesh=mesh, in_specs=placed, out_specs=P(("dp", "ctx"), "head"), check_vma=False
    )
```

```python
import functools

import jax
import jax.numpy as jnp
import numpy as np
from jax import lax
from jax.experimental import pallas as pl
from jax.experimental.pallas import tpu as pltpu
from jax.sharding import PartitionSpec as P

HD = 128
GROUP = 4
ROWS = 256
BROW = 8
NCTX = 32
NHEAD = 4
NDOCS = 16
FEAT = 1024
BEHIND = 8
ROPE_BASE = 500000.0
MASKED = -1e30
MESH = pl.DeviceIdType.MESH

SHIFT = 2
CHUNKS = 8
DEPTH = 4
LAG_OPP = 3

R = ROWS // CHUNKS
BACKWARD = SHIFT
FORWARD = BEHIND // 2 - SHIFT
GROUPS = CHUNKS // 2
OWN = BEHIND - 2 * SHIFT
QROWS = GROUP * ROWS
GROWS = 2 * R
PARTS = 2
BLOCK = GROUP * BROW
ROUNDS = NCTX // 4 - 1
EXPC = float(np.log2(np.e) / np.sqrt(HD))

F32 = jnp.float32
BF16 = jnp.bfloat16


def when(cond):
    if isinstance(cond, (bool, np.bool_)):
        return (lambda f: f()) if cond else (lambda f: None)
    return pl.when(cond)


def both(*conds):
    out = True
    for c in conds:
        if isinstance(c, (bool, np.bool_)):
            if not c:
                return False
        else:
            out = c if out is True else jnp.logical_and(out, c)
    return out


def kernel(
    tokens, query, w_key, w_value, lengths, balance, freq, out,
    gath, wkv, part, cosf, sinf, kv, qbuf, q2, qidx, mx, tot, acc, stage, recv,
    local_sem, tsend, trecv, zsend, zrecv, srecv, qsend, qrecv, osend, orecv, round_sem,
):
    x = lax.axis_index("dp")
    me = lax.axis_index("ctx")
    y = lax.axis_index("head")
    z = me // 2
    core = lax.rem(me, 2)
    up = lax.rem(y + 1, NHEAD)
    down = lax.rem(y + NHEAD - 1, NHEAD)
    opposite = lax.rem(y + 2, NHEAD)
    sibling = me + 1 - 2 * core
    qshard = lax.rem(me + 2 * SHIFT, NCTX)

    def remote(src, dst, ssem, rsem, ctx, head):
        return pltpu.make_async_remote_copy(
            src_ref=src, dst_ref=dst, send_sem=ssem, recv_sem=rsem,
            device_id=(x, ctx, head), device_id_type=MESH,
        )

    def own_copy(c, p):
        rows = pl.ds(c * R, R)
        return remote(
            tokens.at[rows, :], gath.at[1 + p, rows, :], tsend.at[0], trecv.at[p, c],
            me, up if p == 0 else down,
        )

    def relay_copy(c, p):
        rows = pl.ds(c * R + p * (R // 2), R // 2)
        return remote(
            gath.at[1 + p, rows, :], gath.at[3, rows, :], tsend.at[0], trecv.at[2 + p, c],
            me, up if p == 0 else down,
        )

    def slot(u, start, size):
        return kv.at[u, pl.ds(pl.multiple_of(start, size), size), pl.ds(0, 2 * HD)]

    def hop_copy(c, sign, h):
        index = h - 1 if sign > 0 else FORWARD + h - 1
        return remote(
            slot(OWN, c * R, R), slot(OWN - sign * 2 * h, c * R, R),
            zsend.at[0], zrecv.at[index, c // 2], lax.rem(me + NCTX + sign * 2 * h, NCTX), y,
        )

    def hop_wait(g, sign, h):
        index = h - 1 if sign > 0 else FORWARD + h - 1
        here = slot(OWN - sign * 2 * h, g * GROWS, GROWS)
        pltpu.make_async_copy(here, here, zrecv.at[index, g]).wait()

    def sib_start(g, u):
        def start():
            remote(
                slot(u, g * GROWS, GROWS), slot(u - 1 + 2 * core, g * GROWS, GROWS),
                zsend.at[0], srecv.at[u // 2 - 1 + core, g], sibling, y,
            ).start()

        if u == 0:
            pl.when(core == 1)(start)
        elif u == BEHIND:
            pl.when(core == 0)(start)
        else:
            start()

    def sib_arrived(g):
        for k in range(BEHIND // 2):
            here = slot(2 * k + 1, g * GROWS, GROWS)
            pltpu.make_async_copy(here, here, srecv.at[k, g]).wait()

    def hops(g):
        sib_start(g, OWN)
        for h in range(1, max(FORWARD, BACKWARD) + 1):
            for sign, count in ((1, FORWARD), (-1, BACKWARD)):
                if h <= count:
                    hop_wait(g, sign, h)
                    sib_start(g, OWN - sign * 2 * h)

    query_copy = remote(
        query, qbuf, qsend.at[0], qrecv.at[0], lax.rem(me + NCTX - 2 * SHIFT, NCTX), y
    )

    barrier = pltpu.get_barrier_semaphore()

    ahead = lax.rem(me + 2, NCTX)
    astern = lax.rem(me + NCTX - 2, NCTX)
    for ctx, head in ((me, up), (me, down), (ahead, y), (astern, y), (sibling, y)):
        pl.semaphore_signal(barrier, inc=1, device_id=(x, ctx, head), device_id_type=MESH)

    def tell(k):
        for ctx in (ahead, astern):
            pl.semaphore_signal(
                round_sem.at[k], inc=1, device_id=(x, ctx, y), device_id_type=MESH
            )

    loads = [
        pltpu.make_async_copy(tokens, gath.at[0], local_sem.at[0]),
        pltpu.make_async_copy(w_value, wkv.at[:, pl.ds(0, HD)], local_sem.at[1]),
        pltpu.make_async_copy(w_key, wkv.at[:, pl.ds(HD, HD)], local_sem.at[2]),
    ]
    if SHIFT == 0:
        loads.append(pltpu.make_async_copy(query, qbuf, local_sem.at[3]))
    for load in loads:
        load.start()

    pl.semaphore_wait(barrier, 5)

    for c in range(DEPTH):
        for p in range(2):
            own_copy(c, p).start()
    tell(0)

    lane = lax.broadcasted_iota(jnp.int32, (1, HD), 1)
    low = jnp.zeros((1, HD), jnp.int32)
    high = jnp.zeros((1, HD), jnp.int32)
    edge = jnp.int32(0)
    for j in range(NDOCS):
        low = jnp.where(lane == j, edge, low)
        edge = edge + lengths[j]
        high = jnp.where(lane == j, edge, high)

    def in_doc(pos):
        return (pos >= low) & (pos < high)

    pos = me * ROWS + lax.broadcasted_iota(jnp.int32, (ROWS, HD), 0)
    angle = pos.astype(F32) * freq[...]
    cosf[...] = jnp.cos(angle)
    sine = jnp.sin(angle)
    sinf[...] = jnp.where(lax.broadcasted_iota(jnp.int32, (ROWS, HD), 1) < HD // 2, -sine, sine)

    def mark(u, carry):
        shard = (me + NCTX - BEHIND + 2 * SHIFT + u) & (NCTX - 1)
        kpos = shard * ROWS + lax.broadcasted_iota(jnp.int32, (ROWS, HD), 0)
        kv[u, :, pl.ds(2 * HD, HD)] = jnp.where(in_doc(kpos), 0.0, MASKED).astype(BF16)
        return carry

    lax.fori_loop(0, BEHIND + 1, mark, 0)
    qpos = qshard * ROWS + lax.broadcasted_iota(jnp.int32, (ROWS, HD), 0)

    mx[...] = jnp.full_like(mx, MASKED)
    tot[...] = jnp.zeros_like(tot)
    acc[...] = jnp.zeros_like(acc)
    for load in loads:
        load.wait()

    def dest_of(n, e):
        if isinstance(n, int):
            dz = 8 - n if e < 2 else (0 if n == 0 else n - 8)
        else:
            dz = 8 - n if e < 2 else jnp.where(n == 0, 0, n - 8)
        return ((z + 16 + dz) & 15) * 2 + ((core + e) & 1)

    def prepare_query():
        if SHIFT:
            query_copy.wait_recv()
        r = lax.broadcasted_iota(jnp.int32, (ROWS, NCTX), 0)
        n = r >> 5
        e = (r >> 3) & 3
        dz = jnp.where(e < 2, 8 - n, jnp.where(n == 0, 0, n - 8))
        dest = ((z + 16 + dz) & 15) * 2 + ((core + e) & 1)
        bal = balance[pl.ds(qshard, 1), :]
        pick = jnp.where(bal == dest, 1.0, 0.0).astype(BF16)
        b = lax.broadcasted_iota(jnp.int32, (NCTX, ROWS), 0)
        c = lax.broadcasted_iota(jnp.int32, (NCTX, ROWS), 1)
        widen = jnp.where((c >> 3) == b, 1.0, 0.0).astype(BF16)
        spread = jnp.dot(pick, widen, preferred_element_type=F32)
        r = lax.broadcasted_iota(jnp.int32, (ROWS, ROWS), 0)
        c = lax.broadcasted_iota(jnp.int32, (ROWS, ROWS), 1)
        perm = jnp.where((c & 7) == (r & 7), spread, 0.0).astype(BF16)
        moved = jnp.dot(perm, qbuf[...], preferred_element_type=F32)
        doc = jnp.where(in_doc(qpos), 1.0, 0.0).astype(BF16)
        doc = jnp.dot(perm, doc, preferred_element_type=F32)
        index = lax.broadcasted_iota(jnp.int32, (ROWS, HD), 0).astype(F32).astype(BF16)
        index = jnp.dot(perm, index, preferred_element_type=F32)

        def rows_of(parts):
            parts = [p.reshape(NCTX, BROW, HD) for p in parts]
            return jnp.stack(parts, axis=1).reshape(QROWS, HD)

        q2[:, pl.ds(0, HD)] = rows_of(
            [moved[:, g * HD : (g + 1) * HD] for g in range(GROUP)]
        ).astype(BF16)
        q2[:, pl.ds(HD, HD)] = rows_of([doc] * GROUP).astype(BF16)
        qidx[...] = rows_of([index] * GROUP)

    def nt(a, b):
        return lax.dot_general(a, b, (((1,), (1,)), ((), ())), preferred_element_type=F32)

    def attend(g, rows):
        group = pl.ds(g * GROWS, GROWS)
        keys = kv[pl.ds(0, BEHIND), group, pl.ds(HD, 2 * HD)].reshape(BEHIND * GROWS, 2 * HD)
        values = kv[pl.ds(0, BEHIND), group, pl.ds(0, HD)].reshape(BEHIND * GROWS, HD)
        if g % 2:
            start = g // 2 * HD
            half = pl.ds(start, HD)
            keys = jnp.concatenate([keys, kv[BEHIND, half, pl.ds(HD, 2 * HD)]], axis=0)
            values = jnp.concatenate([values, kv[BEHIND, half, pl.ds(0, HD)]], axis=0)
        score = nt(q2[rows, :], keys)
        width = score.shape[1]
        if g % 2:
            index = qidx[rows, :]
            kidx = (start + lax.broadcasted_iota(jnp.int32, index.shape, 1)).astype(F32)
            last = jnp.where(kidx <= index, score[:, width - HD :], MASKED)
            score = jnp.concatenate([score[:, : width - HD], last], axis=1)
        old = mx[rows, :]
        new = jnp.maximum(old, jnp.max(score, axis=1, keepdims=True))
        keep = jnp.exp2((old - new) * EXPC)
        weight = jnp.exp2((score - jnp.concatenate([new] * (width // HD), axis=1)) * EXPC)
        lanes = weight[:, :HD]
        for k in range(1, width // HD):
            lanes = lanes + weight[:, k * HD : (k + 1) * HD]
        mx[rows, :] = new
        tot[rows, :] = tot[rows, :] * keep + lanes
        acc[rows, :] = acc[rows, :] * keep + jnp.dot(
            weight.astype(BF16), values, preferred_element_type=F32
        )

    def out_copy(n, e):
        rows = pl.ds(pl.multiple_of((n * 4 + e) * BLOCK, BLOCK), BLOCK)
        there = pl.ds(pl.multiple_of(qshard * BLOCK, BLOCK), BLOCK)
        return remote(
            stage.at[rows, :], recv.at[there, :], osend.at[0], orecv.at[qshard],
            dest_of(n, e), y,
        )

    def finish(c):
        rows = pl.ds(c * R, R)
        for p in range(2):
            relay_copy(c, p).wait_recv()
        raw = part[rows, :] + jnp.dot(
            gath[3, rows, :], wkv[pl.ds(pl.multiple_of(opposite * FEAT, FEAT), FEAT), :],
            preferred_element_type=F32,
        )
        value = raw[:, :HD]
        key = raw[:, HD:]
        key = key * cosf[rows, :] + pltpu.roll(key, HD // 2, 1) * sinf[rows, :]
        kv[OWN, rows, pl.ds(0, 2 * HD)] = jnp.concatenate([value, key], axis=1).astype(BF16)
        for sign, count in ((1, FORWARD), (-1, BACKWARD)):
            for h in range(1, count + 1):
                hop_copy(c, sign, h).start()

    def gather(i, carry):
        for p in range(2):
            own_copy(i, p).wait_recv()
            relay_copy(i, p).start()

        @pl.when(i + DEPTH < CHUNKS)
        def _():
            for p in range(2):
                own_copy(i + DEPTH, p).start()

        rows = pl.ds(i * R, R)
        total = None
        for s, source in enumerate((y, down, up)):
            term = jnp.dot(
                gath[s, rows, :], wkv[pl.ds(pl.multiple_of(source * FEAT, FEAT), FEAT), :],
                preferred_element_type=F32,
            )
            total = term if total is None else total + term
        part[rows, :] = total

        @pl.when(i >= LAG_OPP)
        def _():
            finish(i - LAG_OPP)

        @pl.when(i < ROUNDS)
        def _():
            pl.semaphore_wait(round_sem.at[i], 2)

        @pl.when(i < ROUNDS - 1)
        def _():
            tell(i + 1)

        if SHIFT:
            @pl.when(i == 0)
            def _():
                query_copy.start()

        @pl.when(i == ROUNDS)
        def _():
            pl.semaphore_signal(
                round_sem.at[ROUNDS], inc=1, device_id=(x, sibling, y), device_id_type=MESH
            )
            pl.semaphore_wait(round_sem.at[ROUNDS], 1)

        return carry

    lax.fori_loop(0, CHUNKS, gather, 0)
    prepare_query()

    def finish_loop(c, carry):
        finish(c)
        return carry

    every = pl.ds(0, QROWS)
    lax.fori_loop(CHUNKS - LAG_OPP, CHUNKS - 1, finish_loop, 0)
    hops(0)
    finish(CHUNKS - 1)
    hops(1)
    sib_arrived(0)
    attend(0, every)
    hops(2)
    sib_arrived(1)
    attend(1, every)
    hops(3)
    sib_arrived(2)
    attend(2, every)
    sib_arrived(3)

    def send(rb, carry):
        for e in range(4):
            if e == 2:
                @pl.when(rb > 0)
                def _():
                    out_copy(rb, e).start()
            else:
                out_copy(rb, e).start()
        return carry

    for p in range(PARTS):
        rows = pl.ds(p * (QROWS // PARTS), QROWS // PARTS)
        attend(3, rows)
        total = jnp.sum(tot[rows, :], axis=1, keepdims=True)
        stage[rows, :] = (acc[rows, :] / total).astype(BF16)
        lax.fori_loop(p * (8 // PARTS), (p + 1) * (8 // PARTS), send, 0)

    def sent(block, sem):
        pltpu.make_async_copy(block, block, sem).wait()

    sent(gath.at[pl.ds(0, 3)], tsend.at[0])
    sent(gath.at[pl.ds(0, 2)], zsend.at[0])
    if SHIFT:
        query_copy.wait_send()

    def arrive(dz, own):
        source = (z + 16 + dz) & 15
        chip = (source + SHIFT) & 15
        for k in range(2):
            shard = chip * 2 + k
            there = pl.ds(pl.multiple_of(shard * BLOCK, BLOCK), BLOCK)

            def landed():
                remote(
                    stage.at[pl.ds(0, BLOCK), :], recv.at[there, :], osend.at[0], orecv.at[shard],
                    sibling, y,
                ).wait_recv()

            if own:
                pl.when(core != k)(landed)
            else:
                landed()
        if own:
            there = pl.ds(pl.multiple_of(qshard * BLOCK, BLOCK), BLOCK)
            recv[there, :] = stage[pl.ds(2 * BLOCK, BLOCK), :]
        block = recv[pl.ds(pl.multiple_of(chip * 2 * BLOCK, 2 * BLOCK), 2 * BLOCK), :].astype(F32)
        heads = [
            jnp.concatenate(
                [
                    block[g * BROW : (g + 1) * BROW],
                    block[BLOCK + g * BROW : BLOCK + (g + 1) * BROW],
                ],
                axis=0,
            )
            for g in range(GROUP)
        ]
        out[pl.ds(pl.multiple_of(chip * 2 * BROW, 2 * BROW), 2 * BROW), :] = jnp.concatenate(
            heads, axis=1
        ).astype(BF16)

    arrive(0, True)
    arrive(8, False)

    def pair(n, carry):
        arrive(8 - n, False)
        arrive(n - 8, False)
        return carry

    lax.fori_loop(1, 8, pair, 0)

    sent(stage.at[pl.ds(0, QROWS - BLOCK), :], osend.at[0])


def local(tokens, query, w_key, w_value, doc_lengths, balance):
    half = HD // 2
    freq = ROPE_BASE ** (-(jnp.arange(half, dtype=F32) * 2.0 / HD))
    freq = jnp.concatenate([freq, freq])[None, :]
    hbm = pl.BlockSpec(memory_space=pltpu.HBM)
    vmem = pl.BlockSpec(memory_space=pltpu.VMEM)
    smem = pl.BlockSpec(memory_space=pltpu.SMEM)
    dma = pltpu.SemaphoreType.DMA
    width = 2 * HD
    return pl.pallas_call(
        kernel,
        out_shape=jax.ShapeDtypeStruct((ROWS, GROUP * HD), BF16),
        in_specs=[hbm, hbm, hbm, hbm, smem, vmem, vmem],
        out_specs=vmem,
        scratch_shapes=[
            pltpu.VMEM((NHEAD, ROWS, FEAT), BF16),
            pltpu.VMEM((NHEAD * FEAT, width), BF16),
            pltpu.VMEM((ROWS, width), F32),
            pltpu.VMEM((ROWS, HD), F32),
            pltpu.VMEM((ROWS, HD), F32),
            pltpu.VMEM((BEHIND + 1, ROWS, 3 * HD), BF16),
            pltpu.VMEM((ROWS, GROUP * HD), BF16),
            pltpu.VMEM((QROWS, width), BF16),
            pltpu.VMEM((QROWS, HD), F32),
            pltpu.VMEM((QROWS, HD), F32),
            pltpu.VMEM((QROWS, HD), F32),
            pltpu.VMEM((QROWS, HD), F32),
            pltpu.VMEM((QROWS, HD), BF16),
            pltpu.VMEM((QROWS, HD), BF16),
            dma((4,)),
            dma((1,)),
            dma((4, CHUNKS)),
            dma((1,)),
            dma((FORWARD + BACKWARD, GROUPS)),
            dma((BEHIND // 2, GROUPS)),
            dma((1,)),
            dma((1,)),
            dma((1,)),
            dma((NCTX,)),
            pltpu.SemaphoreType.REGULAR((ROUNDS + 1,)),
        ],
        compiler_params=pltpu.CompilerParams(
            collective_id=0, has_side_effects=True, vmem_limit_bytes=60 * 1024 * 1024
        ),
        name="attend",
    )(tokens, query, w_key, w_value, doc_lengths, balance, freq)


def solution(mesh):
    placed = (
        P(("dp", "ctx"), "head"),
        P(("dp", "ctx"), "head"),
        P(None, "head"),
        P(None, "head"),
        P("dp"),
        P("dp", None),
    )
    return jax.shard_map(
        local, mesh=mesh, in_specs=placed, out_specs=P(("dp", "ctx"), "head"), check_vma=False
    )
```

```python
import functools

import jax
import jax.numpy as jnp
import numpy as np
from jax import lax
from jax.experimental import pallas as pl
from jax.experimental.pallas import tpu as pltpu
from jax.sharding import PartitionSpec as P

HD = 128
GROUP = 4
ROWS = 256
BROW = 8
NCTX = 32
NHEAD = 4
NDOCS = 16
FEAT = 1024
BEHIND = 8
ROPE_BASE = 500000.0
MASKED = -1e30
MESH = pl.DeviceIdType.MESH

SHIFT = 2
CHUNKS = 8
DEPTH = 4
LAG_OPP = 3

R = ROWS // CHUNKS
BACKWARD = SHIFT
FORWARD = BEHIND // 2 - SHIFT
GROUPS = CHUNKS // 2
OWN = BEHIND - 2 * SHIFT
QROWS = GROUP * ROWS
GROWS = 2 * R
PARTS = 2
BLOCK = GROUP * BROW
ROUNDS = NCTX // 4 - 1
FREQS = (ROPE_BASE ** (-(np.arange(HD // 2) * 2.0 / HD))).astype(np.float32)
EXPC = float(np.log2(np.e) / np.sqrt(HD))

F32 = jnp.float32
BF16 = jnp.bfloat16


def when(cond):
    if isinstance(cond, (bool, np.bool_)):
        return (lambda f: f()) if cond else (lambda f: None)
    return pl.when(cond)


def both(*conds):
    out = True
    for c in conds:
        if isinstance(c, (bool, np.bool_)):
            if not c:
                return False
        else:
            out = c if out is True else jnp.logical_and(out, c)
    return out


def kernel(
    tokens, query, w_key, w_value, lengths_hbm, balance_hbm, out,
    gath, wkv, part, cosf, sinf, kv, qbuf, q2, qidx, mx, tot, acc, stage, recv,
    local_sem, tsend, trecv, zsend, zrecv, srecv, qsend, qrecv, osend, orecv, round_sem, outv, lengths, balance,
):
    x = lax.axis_index("dp")
    me = lax.axis_index("ctx")
    y = lax.axis_index("head")
    z = me // 2
    core = lax.rem(me, 2)
    up = lax.rem(y + 1, NHEAD)
    down = lax.rem(y + NHEAD - 1, NHEAD)
    opposite = lax.rem(y + 2, NHEAD)
    sibling = me + 1 - 2 * core
    qshard = lax.rem(me + 2 * SHIFT, NCTX)

    def remote(src, dst, ssem, rsem, ctx, head):
        return pltpu.make_async_remote_copy(
            src_ref=src, dst_ref=dst, send_sem=ssem, recv_sem=rsem,
            device_id=(x, ctx, head), device_id_type=MESH,
        )

    def own_copy(c, p):
        rows = pl.ds(c * R, R)
        return remote(
            tokens.at[rows, :], gath.at[1 + p, rows, :], tsend.at[0], trecv.at[p, c],
            me, up if p == 0 else down,
        )

    def relay_copy(c, p):
        rows = pl.ds(c * R + p * (R // 2), R // 2)
        return remote(
            gath.at[1 + p, rows, :], gath.at[3, rows, :], tsend.at[0], trecv.at[2 + p, c],
            me, up if p == 0 else down,
        )

    def slot(u, start, size):
        return kv.at[u, pl.ds(pl.multiple_of(start, size), size), pl.ds(0, 2 * HD)]

    def hop_copy(c, sign, h):
        index = h - 1 if sign > 0 else FORWARD + h - 1
        return remote(
            slot(OWN, c * R, R), slot(OWN - sign * 2 * h, c * R, R),
            zsend.at[0], zrecv.at[index, c // 2], lax.rem(me + NCTX + sign * 2 * h, NCTX), y,
        )

    def hop_wait(g, sign, h):
        index = h - 1 if sign > 0 else FORWARD + h - 1
        here = slot(OWN - sign * 2 * h, g * GROWS, GROWS)
        pltpu.make_async_copy(here, here, zrecv.at[index, g]).wait()

    def sib_start(g, u):
        def start():
            remote(
                slot(u, g * GROWS, GROWS), slot(u - 1 + 2 * core, g * GROWS, GROWS),
                zsend.at[0], srecv.at[u // 2 - 1 + core, g], sibling, y,
            ).start()

        if u == 0:
            pl.when(core == 1)(start)
        elif u == BEHIND:
            pl.when(core == 0)(start)
        else:
            start()

    def sib_arrived(g):
        for k in range(BEHIND // 2):
            here = slot(2 * k + 1, g * GROWS, GROWS)
            pltpu.make_async_copy(here, here, srecv.at[k, g]).wait()

    def hops(g):
        sib_start(g, OWN)
        for h in range(1, max(FORWARD, BACKWARD) + 1):
            for sign, count in ((1, FORWARD), (-1, BACKWARD)):
                if h <= count:
                    hop_wait(g, sign, h)
                    sib_start(g, OWN - sign * 2 * h)

    query_copy = remote(
        query, qbuf, qsend.at[0], qrecv.at[0], lax.rem(me + NCTX - 2 * SHIFT, NCTX), y
    )

    barrier = pltpu.get_barrier_semaphore()

    ahead = lax.rem(me + 2, NCTX)
    astern = lax.rem(me + NCTX - 2, NCTX)
    for ctx, head in ((me, up), (me, down), (ahead, y), (astern, y), (sibling, y)):
        pl.semaphore_signal(barrier, inc=1, device_id=(x, ctx, head), device_id_type=MESH)

    def tell(k):
        for ctx in (ahead, astern):
            pl.semaphore_signal(
                round_sem.at[k], inc=1, device_id=(x, ctx, y), device_id_type=MESH
            )

    loads = [
        pltpu.make_async_copy(lengths_hbm, lengths, local_sem.at[4]),
        pltpu.make_async_copy(balance_hbm, balance, local_sem.at[5]),
        pltpu.make_async_copy(tokens, gath.at[0], local_sem.at[0]),
        pltpu.make_async_copy(w_value, wkv.at[:, pl.ds(0, HD)], local_sem.at[1]),
        pltpu.make_async_copy(w_key, wkv.at[:, pl.ds(HD, HD)], local_sem.at[2]),
    ]
    if SHIFT == 0:
        loads.append(pltpu.make_async_copy(query, qbuf, local_sem.at[3]))
    for load in loads:
        load.start()

    pl.semaphore_wait(barrier, 5)

    for c in range(DEPTH):
        for p in range(2):
            own_copy(c, p).start()
    tell(0)

    for load in loads[:2]:
        load.wait()
    lane = lax.broadcasted_iota(jnp.int32, (1, HD), 1)
    low = jnp.zeros((1, HD), jnp.int32)
    high = jnp.zeros((1, HD), jnp.int32)
    edge = jnp.int32(0)
    for j in range(NDOCS):
        low = jnp.where(lane == j, edge, low)
        edge = edge + lengths[j]
        high = jnp.where(lane == j, edge, high)

    def in_doc(pos):
        return (pos >= low) & (pos < high)

    pos = me * ROWS + lax.broadcasted_iota(jnp.int32, (ROWS, HD), 0)
    freq = jnp.zeros((1, HD), F32)
    for j in range(HD // 2):
        freq = jnp.where((lane & (HD // 2 - 1)) == j, float(FREQS[j]), freq)
    angle = pos.astype(F32) * freq
    cosf[...] = jnp.cos(angle)
    sine = jnp.sin(angle)
    sinf[...] = jnp.where(lax.broadcasted_iota(jnp.int32, (ROWS, HD), 1) < HD // 2, -sine, sine)

    def mark(u, carry):
        shard = (me + NCTX - BEHIND + 2 * SHIFT + u) & (NCTX - 1)
        kpos = shard * ROWS + lax.broadcasted_iota(jnp.int32, (ROWS, HD), 0)
        kv[u, :, pl.ds(2 * HD, HD)] = jnp.where(in_doc(kpos), 0.0, MASKED).astype(BF16)
        return carry

    lax.fori_loop(0, BEHIND + 1, mark, 0)
    qpos = qshard * ROWS + lax.broadcasted_iota(jnp.int32, (ROWS, HD), 0)

    mx[...] = jnp.full_like(mx, MASKED)
    tot[...] = jnp.zeros_like(tot)
    acc[...] = jnp.zeros_like(acc)
    for load in loads[2:]:
        load.wait()

    def dest_of(n, e):
        if isinstance(n, int):
            dz = 8 - n if e < 2 else (0 if n == 0 else n - 8)
        else:
            dz = 8 - n if e < 2 else jnp.where(n == 0, 0, n - 8)
        return ((z + 16 + dz) & 15) * 2 + ((core + e) & 1)

    def prepare_query():
        if SHIFT:
            query_copy.wait_recv()
        r = lax.broadcasted_iota(jnp.int32, (ROWS, NCTX), 0)
        n = r >> 5
        e = (r >> 3) & 3
        dz = jnp.where(e < 2, 8 - n, jnp.where(n == 0, 0, n - 8))
        dest = ((z + 16 + dz) & 15) * 2 + ((core + e) & 1)
        bal = balance[pl.ds(qshard, 1), :]
        pick = jnp.where(bal == dest, 1.0, 0.0).astype(BF16)
        b = lax.broadcasted_iota(jnp.int32, (NCTX, ROWS), 0)
        c = lax.broadcasted_iota(jnp.int32, (NCTX, ROWS), 1)
        widen = jnp.where((c >> 3) == b, 1.0, 0.0).astype(BF16)
        spread = jnp.dot(pick, widen, preferred_element_type=F32)
        r = lax.broadcasted_iota(jnp.int32, (ROWS, ROWS), 0)
        c = lax.broadcasted_iota(jnp.int32, (ROWS, ROWS), 1)
        perm = jnp.where((c & 7) == (r & 7), spread, 0.0).astype(BF16)
        moved = jnp.dot(perm, qbuf[...], preferred_element_type=F32)
        doc = jnp.where(in_doc(qpos), 1.0, 0.0).astype(BF16)
        doc = jnp.dot(perm, doc, preferred_element_type=F32)
        index = lax.broadcasted_iota(jnp.int32, (ROWS, HD), 0).astype(F32).astype(BF16)
        index = jnp.dot(perm, index, preferred_element_type=F32)

        def rows_of(parts):
            parts = [p.reshape(NCTX, BROW, HD) for p in parts]
            return jnp.stack(parts, axis=1).reshape(QROWS, HD)

        q2[:, pl.ds(0, HD)] = rows_of(
            [moved[:, g * HD : (g + 1) * HD] for g in range(GROUP)]
        ).astype(BF16)
        q2[:, pl.ds(HD, HD)] = rows_of([doc] * GROUP).astype(BF16)
        qidx[...] = rows_of([index] * GROUP)

    def nt(a, b):
        return lax.dot_general(a, b, (((1,), (1,)), ((), ())), preferred_element_type=F32)

    def attend(g, rows):
        group = pl.ds(g * GROWS, GROWS)
        keys = kv[pl.ds(0, BEHIND), group, pl.ds(HD, 2 * HD)].reshape(BEHIND * GROWS, 2 * HD)
        values = kv[pl.ds(0, BEHIND), group, pl.ds(0, HD)].reshape(BEHIND * GROWS, HD)
        if g % 2:
            start = g // 2 * HD
            half = pl.ds(start, HD)
            keys = jnp.concatenate([keys, kv[BEHIND, half, pl.ds(HD, 2 * HD)]], axis=0)
            values = jnp.concatenate([values, kv[BEHIND, half, pl.ds(0, HD)]], axis=0)
        score = nt(q2[rows, :], keys)
        width = score.shape[1]
        if g % 2:
            index = qidx[rows, :]
            kidx = (start + lax.broadcasted_iota(jnp.int32, index.shape, 1)).astype(F32)
            last = jnp.where(kidx <= index, score[:, width - HD :], MASKED)
            score = jnp.concatenate([score[:, : width - HD], last], axis=1)
        old = mx[rows, :]
        new = jnp.maximum(old, jnp.max(score, axis=1, keepdims=True))
        keep = jnp.exp2((old - new) * EXPC)
        weight = jnp.exp2((score - jnp.concatenate([new] * (width // HD), axis=1)) * EXPC)
        lanes = weight[:, :HD]
        for k in range(1, width // HD):
            lanes = lanes + weight[:, k * HD : (k + 1) * HD]
        mx[rows, :] = new
        tot[rows, :] = tot[rows, :] * keep + lanes
        acc[rows, :] = acc[rows, :] * keep + jnp.dot(
            weight.astype(BF16), values, preferred_element_type=F32
        )

    def out_copy(n, e):
        rows = pl.ds(pl.multiple_of((n * 4 + e) * BLOCK, BLOCK), BLOCK)
        there = pl.ds(pl.multiple_of(qshard * BLOCK, BLOCK), BLOCK)
        return remote(
            stage.at[rows, :], recv.at[there, :], osend.at[0], orecv.at[qshard],
            dest_of(n, e), y,
        )

    def finish(c):
        rows = pl.ds(c * R, R)
        for p in range(2):
            relay_copy(c, p).wait_recv()
        raw = part[rows, :] + jnp.dot(
            gath[3, rows, :], wkv[pl.ds(pl.multiple_of(opposite * FEAT, FEAT), FEAT), :],
            preferred_element_type=F32,
        )
        value = raw[:, :HD]
        key = raw[:, HD:]
        key = key * cosf[rows, :] + pltpu.roll(key, HD // 2, 1) * sinf[rows, :]
        kv[OWN, rows, pl.ds(0, 2 * HD)] = jnp.concatenate([value, key], axis=1).astype(BF16)
        for sign, count in ((1, FORWARD), (-1, BACKWARD)):
            for h in range(1, count + 1):
                hop_copy(c, sign, h).start()

    def gather(i, carry):
        for p in range(2):
            own_copy(i, p).wait_recv()
            relay_copy(i, p).start()

        @pl.when(i + DEPTH < CHUNKS)
        def _():
            for p in range(2):
                own_copy(i + DEPTH, p).start()

        rows = pl.ds(i * R, R)
        total = None
        for s, source in enumerate((y, down, up)):
            term = jnp.dot(
                gath[s, rows, :], wkv[pl.ds(pl.multiple_of(source * FEAT, FEAT), FEAT), :],
                preferred_element_type=F32,
            )
            total = term if total is None else total + term
        part[rows, :] = total

        @pl.when(i >= LAG_OPP)
        def _():
            finish(i - LAG_OPP)

        @pl.when(i < ROUNDS)
        def _():
            pl.semaphore_wait(round_sem.at[i], 2)

        @pl.when(i < ROUNDS - 1)
        def _():
            tell(i + 1)

        if SHIFT:
            @pl.when(i == 0)
            def _():
                query_copy.start()

        @pl.when(i == ROUNDS)
        def _():
            pl.semaphore_signal(
                round_sem.at[ROUNDS], inc=1, device_id=(x, sibling, y), device_id_type=MESH
            )
            pl.semaphore_wait(round_sem.at[ROUNDS], 1)

        return carry

    lax.fori_loop(0, CHUNKS, gather, 0)
    prepare_query()

    def finish_loop(c, carry):
        finish(c)
        return carry

    every = pl.ds(0, QROWS)
    lax.fori_loop(CHUNKS - LAG_OPP, CHUNKS - 1, finish_loop, 0)
    hops(0)
    finish(CHUNKS - 1)
    hops(1)
    sib_arrived(0)
    attend(0, every)
    hops(2)
    sib_arrived(1)
    attend(1, every)
    hops(3)
    sib_arrived(2)
    attend(2, every)
    sib_arrived(3)

    def send(rb, carry):
        for e in range(4):
            if e == 2:
                @pl.when(rb > 0)
                def _():
                    out_copy(rb, e).start()
            else:
                out_copy(rb, e).start()
        return carry

    for p in range(PARTS):
        rows = pl.ds(p * (QROWS // PARTS), QROWS // PARTS)
        attend(3, rows)
        total = jnp.sum(tot[rows, :], axis=1, keepdims=True)
        stage[rows, :] = (acc[rows, :] / total).astype(BF16)
        lax.fori_loop(p * (8 // PARTS), (p + 1) * (8 // PARTS), send, 0)

    def sent(block, sem):
        pltpu.make_async_copy(block, block, sem).wait()

    sent(gath.at[pl.ds(0, 3)], tsend.at[0])
    sent(gath.at[pl.ds(0, 2)], zsend.at[0])
    if SHIFT:
        query_copy.wait_send()

    def arrive(dz, own):
        source = (z + 16 + dz) & 15
        chip = (source + SHIFT) & 15
        for k in range(2):
            shard = chip * 2 + k
            there = pl.ds(pl.multiple_of(shard * BLOCK, BLOCK), BLOCK)

            def landed():
                remote(
                    stage.at[pl.ds(0, BLOCK), :], recv.at[there, :], osend.at[0], orecv.at[shard],
                    sibling, y,
                ).wait_recv()

            if own:
                pl.when(core != k)(landed)
            else:
                landed()
        if own:
            there = pl.ds(pl.multiple_of(qshard * BLOCK, BLOCK), BLOCK)
            recv[there, :] = stage[pl.ds(2 * BLOCK, BLOCK), :]
        block = recv[pl.ds(pl.multiple_of(chip * 2 * BLOCK, 2 * BLOCK), 2 * BLOCK), :].astype(F32)
        heads = [
            jnp.concatenate(
                [
                    block[g * BROW : (g + 1) * BROW],
                    block[BLOCK + g * BROW : BLOCK + (g + 1) * BROW],
                ],
                axis=0,
            )
            for g in range(GROUP)
        ]
        final = pl.ds(pl.multiple_of(chip * 2 * BROW, 2 * BROW), 2 * BROW)
        outv[final, :] = jnp.concatenate(heads, axis=1).astype(BF16)
        pltpu.make_async_copy(outv.at[final, :], out.at[final, :], local_sem.at[3]).start()

    arrive(0, True)
    arrive(8, False)

    def pair(n, carry):
        arrive(8 - n, False)
        arrive(n - 8, False)
        return carry

    lax.fori_loop(1, 8, pair, 0)

    sent(stage.at[pl.ds(0, QROWS - BLOCK), :], osend.at[0])
    sent(outv, local_sem.at[3])


def local(tokens, query, w_key, w_value, doc_lengths, balance):
    hbm = pl.BlockSpec(memory_space=pltpu.HBM)
    dma = pltpu.SemaphoreType.DMA
    width = 2 * HD
    return pl.pallas_call(
        kernel,
        out_shape=jax.ShapeDtypeStruct((ROWS, GROUP * HD), BF16),
        in_specs=[hbm] * 6,
        out_specs=hbm,
        scratch_shapes=[
            pltpu.VMEM((NHEAD, ROWS, FEAT), BF16),
            pltpu.VMEM((NHEAD * FEAT, width), BF16),
            pltpu.VMEM((ROWS, width), F32),
            pltpu.VMEM((ROWS, HD), F32),
            pltpu.VMEM((ROWS, HD), F32),
            pltpu.VMEM((BEHIND + 1, ROWS, 3 * HD), BF16),
            pltpu.VMEM((ROWS, GROUP * HD), BF16),
            pltpu.VMEM((QROWS, width), BF16),
            pltpu.VMEM((QROWS, HD), F32),
            pltpu.VMEM((QROWS, HD), F32),
            pltpu.VMEM((QROWS, HD), F32),
            pltpu.VMEM((QROWS, HD), F32),
            pltpu.VMEM((QROWS, HD), BF16),
            pltpu.VMEM((QROWS, HD), BF16),
            dma((6,)),
            dma((1,)),
            dma((4, CHUNKS)),
            dma((1,)),
            dma((FORWARD + BACKWARD, GROUPS)),
            dma((BEHIND // 2, GROUPS)),
            dma((1,)),
            dma((1,)),
            dma((1,)),
            dma((NCTX,)),
            pltpu.SemaphoreType.REGULAR((ROUNDS + 1,)),
            pltpu.VMEM((ROWS, GROUP * HD), BF16),
            pltpu.SMEM((NDOCS,), jnp.int32),
            pltpu.VMEM((NCTX, NCTX), jnp.int32),
        ],
        compiler_params=pltpu.CompilerParams(
            collective_id=0, has_side_effects=True, vmem_limit_bytes=60 * 1024 * 1024
        ),
        name="attend",
    )(tokens, query, w_key, w_value, doc_lengths, balance)


def solution(mesh):
    placed = (
        P(("dp", "ctx"), "head"),
        P(("dp", "ctx"), "head"),
        P(None, "head"),
        P(None, "head"),
        P("dp"),
        P("dp", None),
    )
    return jax.shard_map(
        local, mesh=mesh, in_specs=placed, out_specs=P(("dp", "ctx"), "head"), check_vma=False
    )
```

```python
import functools

import jax
import jax.numpy as jnp
import numpy as np
from jax import lax
from jax.experimental import pallas as pl
from jax.experimental.pallas import tpu as pltpu
from jax.sharding import PartitionSpec as P

HD = 128
GROUP = 4
ROWS = 256
BROW = 8
NCTX = 32
NHEAD = 4
NDOCS = 16
FEAT = 1024
BEHIND = 8
ROPE_BASE = 500000.0
MASKED = -1e30
MESH = pl.DeviceIdType.MESH

SHIFT = 2
CHUNKS = 8
DEPTH = 4
LAG_OPP = 3

R = ROWS // CHUNKS
BACKWARD = SHIFT
FORWARD = BEHIND // 2 - SHIFT
GROUPS = CHUNKS // 2
OWN = BEHIND - 2 * SHIFT
QROWS = GROUP * ROWS
GROWS = 2 * R
PARTS = 2
BLOCK = GROUP * BROW
ROUNDS = NCTX // 4 - 1
FREQS = (ROPE_BASE ** (-(np.arange(HD // 2) * 2.0 / HD))).astype(np.float32)
EXPC = float(np.log2(np.e) / np.sqrt(HD))

F32 = jnp.float32
BF16 = jnp.bfloat16


def when(cond):
    if isinstance(cond, (bool, np.bool_)):
        return (lambda f: f()) if cond else (lambda f: None)
    return pl.when(cond)


def both(*conds):
    out = True
    for c in conds:
        if isinstance(c, (bool, np.bool_)):
            if not c:
                return False
        else:
            out = c if out is True else jnp.logical_and(out, c)
    return out


def kernel(
    tokens, query, w_key, w_value, lengths_hbm, balance_hbm, out,
    gath, wkv, part, cosf, sinf, kv, qbuf, q2, qidx, mx, tot, acc, stage, recv,
    local_sem, tsend, trecv, zsend, zrecv, srecv, qsend, qrecv, osend, orecv, round_sem, outv, lengths, balance,
):
    x = lax.axis_index("dp")
    me = lax.axis_index("ctx")
    y = lax.axis_index("head")
    z = me // 2
    core = lax.rem(me, 2)
    up = lax.rem(y + 1, NHEAD)
    down = lax.rem(y + NHEAD - 1, NHEAD)
    opposite = lax.rem(y + 2, NHEAD)
    sibling = me + 1 - 2 * core
    qshard = lax.rem(me + 2 * SHIFT, NCTX)

    def remote(src, dst, ssem, rsem, ctx, head):
        return pltpu.make_async_remote_copy(
            src_ref=src, dst_ref=dst, send_sem=ssem, recv_sem=rsem,
            device_id=(x, ctx, head), device_id_type=MESH,
        )

    def own_copy(c, p):
        rows = pl.ds(c * R, R)
        return remote(
            tokens.at[rows, :], gath.at[1 + p, rows, :], tsend.at[0], trecv.at[p, c],
            me, up if p == 0 else down,
        )

    def relay_copy(c, p):
        rows = pl.ds(c * R + p * (R // 2), R // 2)
        return remote(
            gath.at[1 + p, rows, :], gath.at[3, rows, :], tsend.at[0], trecv.at[2 + p, c],
            me, up if p == 0 else down,
        )

    def slot(u, start, size):
        return kv.at[u, pl.ds(pl.multiple_of(start, size), size), pl.ds(0, 2 * HD)]

    def hop_copy(c, sign, h):
        index = h - 1 if sign > 0 else FORWARD + h - 1
        return remote(
            slot(OWN, c * R, R), slot(OWN - sign * 2 * h, c * R, R),
            zsend.at[0], zrecv.at[index, c // 2], lax.rem(me + NCTX + sign * 2 * h, NCTX), y,
        )

    def hop_wait(g, sign, h):
        index = h - 1 if sign > 0 else FORWARD + h - 1
        here = slot(OWN - sign * 2 * h, g * GROWS, GROWS)
        pltpu.make_async_copy(here, here, zrecv.at[index, g]).wait()

    def sib_start(g, u):
        def start():
            remote(
                slot(u, g * GROWS, GROWS), slot(u - 1 + 2 * core, g * GROWS, GROWS),
                zsend.at[0], srecv.at[u // 2 - 1 + core, g], sibling, y,
            ).start()

        if u == 0:
            pl.when(core == 1)(start)
        elif u == BEHIND:
            pl.when(core == 0)(start)
        else:
            start()

    def sib_arrived(g):
        for k in range(BEHIND // 2):
            here = slot(2 * k + 1, g * GROWS, GROWS)
            pltpu.make_async_copy(here, here, srecv.at[k, g]).wait()

    def hops(g):
        sib_start(g, OWN)
        for h in range(1, max(FORWARD, BACKWARD) + 1):
            for sign, count in ((1, FORWARD), (-1, BACKWARD)):
                if h <= count:
                    hop_wait(g, sign, h)
                    sib_start(g, OWN - sign * 2 * h)

    query_copy = remote(
        query, qbuf, qsend.at[0], qrecv.at[0], lax.rem(me + NCTX - 2 * SHIFT, NCTX), y
    )

    barrier = pltpu.get_barrier_semaphore()

    ahead = lax.rem(me + 2, NCTX)
    astern = lax.rem(me + NCTX - 2, NCTX)
    for ctx, head in ((me, up), (me, down), (ahead, y), (astern, y), (sibling, y)):
        pl.semaphore_signal(barrier, inc=1, device_id=(x, ctx, head), device_id_type=MESH)

    def tell(k):
        for ctx in (ahead, astern):
            pl.semaphore_signal(
                round_sem.at[k], inc=1, device_id=(x, ctx, y), device_id_type=MESH
            )

    loads = [
        pltpu.make_async_copy(lengths_hbm, lengths, local_sem.at[4]),
        pltpu.make_async_copy(balance_hbm, balance, local_sem.at[5]),
        pltpu.make_async_copy(tokens, gath.at[0], local_sem.at[0]),
        pltpu.make_async_copy(w_value, wkv.at[:, pl.ds(0, HD)], local_sem.at[1]),
        pltpu.make_async_copy(w_key, wkv.at[:, pl.ds(HD, HD)], local_sem.at[2]),
    ]
    if SHIFT == 0:
        loads.append(pltpu.make_async_copy(query, qbuf, local_sem.at[3]))
    for load in loads:
        load.start()

    pl.semaphore_wait(barrier, 5)

    for c in range(DEPTH):
        for p in range(2):
            own_copy(c, p).start()
    tell(0)

    for load in loads[:2]:
        load.wait()
    lane = lax.broadcasted_iota(jnp.int32, (1, HD), 1)
    low = jnp.zeros((1, HD), jnp.int32)
    high = jnp.zeros((1, HD), jnp.int32)
    edge = jnp.int32(0)
    for j in range(NDOCS):
        low = jnp.where(lane == j, edge, low)
        edge = edge + lengths[j]
        high = jnp.where(lane == j, edge, high)

    def in_doc(pos):
        return (pos >= low) & (pos < high)

    pos = me * ROWS + lax.broadcasted_iota(jnp.int32, (ROWS, HD), 0)
    freq = jnp.zeros((1, HD), F32)
    for j in range(HD // 2):
        freq = jnp.where((lane & (HD // 2 - 1)) == j, float(FREQS[j]), freq)
    angle = pos.astype(F32) * freq
    cosf[...] = jnp.cos(angle)
    sine = jnp.sin(angle)
    sinf[...] = jnp.where(lax.broadcasted_iota(jnp.int32, (ROWS, HD), 1) < HD // 2, -sine, sine)

    def mark(u, carry):
        shard = (me + NCTX - BEHIND + 2 * SHIFT + u) & (NCTX - 1)
        kpos = shard * ROWS + lax.broadcasted_iota(jnp.int32, (ROWS, HD), 0)
        kv[u, :, pl.ds(2 * HD, HD)] = jnp.where(in_doc(kpos), 0.0, MASKED).astype(BF16)
        return carry

    lax.fori_loop(0, BEHIND + 1, mark, 0)
    qpos = qshard * ROWS + lax.broadcasted_iota(jnp.int32, (ROWS, HD), 0)

    mx[...] = jnp.full_like(mx, MASKED)
    tot[...] = jnp.zeros_like(tot)
    acc[...] = jnp.zeros_like(acc)
    for load in loads[2:]:
        load.wait()

    def dest_of(n, e):
        if isinstance(n, int):
            dz = 8 - n if e < 2 else (0 if n == 0 else n - 8)
        else:
            dz = 8 - n if e < 2 else jnp.where(n == 0, 0, n - 8)
        return ((z + 16 + dz) & 15) * 2 + ((core + e) & 1)

    def prepare_query():
        if SHIFT:
            query_copy.wait_recv()
        r = lax.broadcasted_iota(jnp.int32, (ROWS, NCTX), 0)
        n = r >> 5
        e = (r >> 3) & 3
        dz = jnp.where(e < 2, 8 - n, jnp.where(n == 0, 0, n - 8))
        dest = ((z + 16 + dz) & 15) * 2 + ((core + e) & 1)
        bal = balance[pl.ds(qshard, 1), :]
        pick = jnp.where(bal == dest, 1.0, 0.0).astype(BF16)
        b = lax.broadcasted_iota(jnp.int32, (NCTX, ROWS), 0)
        c = lax.broadcasted_iota(jnp.int32, (NCTX, ROWS), 1)
        widen = jnp.where((c >> 3) == b, 1.0, 0.0).astype(BF16)
        spread = jnp.dot(pick, widen, preferred_element_type=F32)
        r = lax.broadcasted_iota(jnp.int32, (ROWS, ROWS), 0)
        c = lax.broadcasted_iota(jnp.int32, (ROWS, ROWS), 1)
        perm = jnp.where((c & 7) == (r & 7), spread, 0.0).astype(BF16)
        moved = jnp.dot(perm, qbuf[...], preferred_element_type=F32)
        doc = jnp.where(in_doc(qpos), 1.0, 0.0).astype(BF16)
        doc = jnp.dot(perm, doc, preferred_element_type=F32)
        index = lax.broadcasted_iota(jnp.int32, (ROWS, HD), 0).astype(F32).astype(BF16)
        index = jnp.dot(perm, index, preferred_element_type=F32)

        def rows_of(parts):
            parts = [p.reshape(NCTX, BROW, HD) for p in parts]
            return jnp.stack(parts, axis=1).reshape(QROWS, HD)

        q2[:, pl.ds(0, HD)] = rows_of(
            [moved[:, g * HD : (g + 1) * HD] for g in range(GROUP)]
        ).astype(BF16)
        q2[:, pl.ds(HD, HD)] = rows_of([doc] * GROUP).astype(BF16)
        qidx[...] = rows_of([index] * GROUP)

    def nt(a, b):
        return lax.dot_general(a, b, (((1,), (1,)), ((), ())), preferred_element_type=F32)

    def attend(g, rows):
        group = pl.ds(g * GROWS, GROWS)
        keys = kv[pl.ds(0, BEHIND), group, pl.ds(HD, 2 * HD)].reshape(BEHIND * GROWS, 2 * HD)
        values = kv[pl.ds(0, BEHIND), group, pl.ds(0, HD)].reshape(BEHIND * GROWS, HD)
        if g % 2:
            start = g // 2 * HD
            half = pl.ds(start, HD)
            keys = jnp.concatenate([keys, kv[BEHIND, half, pl.ds(HD, 2 * HD)]], axis=0)
            values = jnp.concatenate([values, kv[BEHIND, half, pl.ds(0, HD)]], axis=0)
        score = nt(q2[rows, :], keys)
        width = score.shape[1]
        if g % 2:
            index = qidx[rows, :]
            kidx = (start + lax.broadcasted_iota(jnp.int32, index.shape, 1)).astype(F32)
            last = jnp.where(kidx <= index, score[:, width - HD :], MASKED)
            score = jnp.concatenate([score[:, : width - HD], last], axis=1)
        old = mx[rows, :]
        new = jnp.maximum(old, jnp.max(score, axis=1, keepdims=True))
        keep = jnp.exp2((old - new) * EXPC)
        weight = jnp.exp2((score - jnp.concatenate([new] * (width // HD), axis=1)) * EXPC)
        lanes = weight[:, :HD]
        for k in range(1, width // HD):
            lanes = lanes + weight[:, k * HD : (k + 1) * HD]
        mx[rows, :] = new
        tot[rows, :] = tot[rows, :] * keep + lanes
        acc[rows, :] = acc[rows, :] * keep + jnp.dot(
            weight.astype(BF16), values, preferred_element_type=F32
        )

    def out_copy(n, e):
        rows = pl.ds(pl.multiple_of((n * 4 + e) * BLOCK, BLOCK), BLOCK)
        there = pl.ds(pl.multiple_of(qshard * BLOCK, BLOCK), BLOCK)
        return remote(
            stage.at[rows, :], recv.at[there, :], osend.at[0], orecv.at[qshard],
            dest_of(n, e), y,
        )

    def finish(c):
        rows = pl.ds(c * R, R)
        for p in range(2):
            relay_copy(c, p).wait_recv()
        raw = part[rows, :] + jnp.dot(
            gath[3, rows, :], wkv[pl.ds(pl.multiple_of(opposite * FEAT, FEAT), FEAT), :],
            preferred_element_type=F32,
        )
        value = raw[:, :HD]
        key = raw[:, HD:]
        key = key * cosf[rows, :] + pltpu.roll(key, HD // 2, 1) * sinf[rows, :]
        kv[OWN, rows, pl.ds(0, 2 * HD)] = jnp.concatenate([value, key], axis=1).astype(BF16)
        for h in range(max(FORWARD, BACKWARD), 0, -1):
            for sign, count in ((1, FORWARD), (-1, BACKWARD)):
                if h <= count:
                    hop_copy(c, sign, h).start()

    def gather(i, carry):
        for p in range(2):
            own_copy(i, p).wait_recv()
            relay_copy(i, p).start()

        @pl.when(i + DEPTH < CHUNKS)
        def _():
            for p in range(2):
                own_copy(i + DEPTH, p).start()

        rows = pl.ds(i * R, R)
        total = None
        for s, source in enumerate((y, down, up)):
            term = jnp.dot(
                gath[s, rows, :], wkv[pl.ds(pl.multiple_of(source * FEAT, FEAT), FEAT), :],
                preferred_element_type=F32,
            )
            total = term if total is None else total + term
        part[rows, :] = total

        @pl.when(i >= LAG_OPP)
        def _():
            finish(i - LAG_OPP)

        @pl.when(i < ROUNDS)
        def _():
            pl.semaphore_wait(round_sem.at[i], 2)

        @pl.when(i < ROUNDS - 1)
        def _():
            tell(i + 1)

        if SHIFT:
            @pl.when(i == 0)
            def _():
                query_copy.start()

        @pl.when(i == ROUNDS)
        def _():
            pl.semaphore_signal(
                round_sem.at[ROUNDS], inc=1, device_id=(x, sibling, y), device_id_type=MESH
            )
            pl.semaphore_wait(round_sem.at[ROUNDS], 1)

        return carry

    lax.fori_loop(0, CHUNKS, gather, 0)
    prepare_query()

    def finish_loop(c, carry):
        finish(c)
        return carry

    every = pl.ds(0, QROWS)
    lax.fori_loop(CHUNKS - LAG_OPP, CHUNKS - 1, finish_loop, 0)
    hops(0)
    finish(CHUNKS - 1)
    hops(1)
    sib_arrived(0)
    attend(0, every)
    hops(2)
    sib_arrived(1)
    attend(1, every)
    hops(3)
    sib_arrived(2)
    attend(2, every)
    sib_arrived(3)

    def send(rb, carry):
        for e in range(4):
            if e == 2:
                @pl.when(rb > 0)
                def _():
                    out_copy(rb, e).start()
            else:
                out_copy(rb, e).start()
        return carry

    for p in range(PARTS):
        rows = pl.ds(p * (QROWS // PARTS), QROWS // PARTS)
        attend(3, rows)
        total = jnp.sum(tot[rows, :], axis=1, keepdims=True)
        stage[rows, :] = (acc[rows, :] / total).astype(BF16)
        lax.fori_loop(p * (8 // PARTS), (p + 1) * (8 // PARTS), send, 0)

    def sent(block, sem):
        pltpu.make_async_copy(block, block, sem).wait()

    sent(gath.at[pl.ds(0, 3)], tsend.at[0])
    sent(gath.at[pl.ds(0, 2)], zsend.at[0])
    if SHIFT:
        query_copy.wait_send()

    def arrive(dz, own):
        source = (z + 16 + dz) & 15
        chip = (source + SHIFT) & 15
        for k in range(2):
            shard = chip * 2 + k
            there = pl.ds(pl.multiple_of(shard * BLOCK, BLOCK), BLOCK)

            def landed():
                remote(
                    stage.at[pl.ds(0, BLOCK), :], recv.at[there, :], osend.at[0], orecv.at[shard],
                    sibling, y,
                ).wait_recv()

            if own:
                pl.when(core != k)(landed)
            else:
                landed()
        if own:
            there = pl.ds(pl.multiple_of(qshard * BLOCK, BLOCK), BLOCK)
            recv[there, :] = stage[pl.ds(2 * BLOCK, BLOCK), :]
        block = recv[pl.ds(pl.multiple_of(chip * 2 * BLOCK, 2 * BLOCK), 2 * BLOCK), :].astype(F32)
        heads = [
            jnp.concatenate(
                [
                    block[g * BROW : (g + 1) * BROW],
                    block[BLOCK + g * BROW : BLOCK + (g + 1) * BROW],
                ],
                axis=0,
            )
            for g in range(GROUP)
        ]
        final = pl.ds(pl.multiple_of(chip * 2 * BROW, 2 * BROW), 2 * BROW)
        outv[final, :] = jnp.concatenate(heads, axis=1).astype(BF16)
        pltpu.make_async_copy(outv.at[final, :], out.at[final, :], local_sem.at[3]).start()

    arrive(0, True)
    arrive(8, False)

    def pair(n, carry):
        arrive(8 - n, False)
        arrive(n - 8, False)
        return carry

    lax.fori_loop(1, 8, pair, 0)

    sent(stage.at[pl.ds(0, QROWS - BLOCK), :], osend.at[0])
    sent(outv, local_sem.at[3])


def local(tokens, query, w_key, w_value, doc_lengths, balance):
    hbm = pl.BlockSpec(memory_space=pltpu.HBM)
    dma = pltpu.SemaphoreType.DMA
    width = 2 * HD
    return pl.pallas_call(
        kernel,
        out_shape=jax.ShapeDtypeStruct((ROWS, GROUP * HD), BF16),
        in_specs=[hbm] * 6,
        out_specs=hbm,
        scratch_shapes=[
            pltpu.VMEM((NHEAD, ROWS, FEAT), BF16),
            pltpu.VMEM((NHEAD * FEAT, width), BF16),
            pltpu.VMEM((ROWS, width), F32),
            pltpu.VMEM((ROWS, HD), F32),
            pltpu.VMEM((ROWS, HD), F32),
            pltpu.VMEM((BEHIND + 1, ROWS, 3 * HD), BF16),
            pltpu.VMEM((ROWS, GROUP * HD), BF16),
            pltpu.VMEM((QROWS, width), BF16),
            pltpu.VMEM((QROWS, HD), F32),
            pltpu.VMEM((QROWS, HD), F32),
            pltpu.VMEM((QROWS, HD), F32),
            pltpu.VMEM((QROWS, HD), F32),
            pltpu.VMEM((QROWS, HD), BF16),
            pltpu.VMEM((QROWS, HD), BF16),
            dma((6,)),
            dma((1,)),
            dma((4, CHUNKS)),
            dma((1,)),
            dma((FORWARD + BACKWARD, GROUPS)),
            dma((BEHIND // 2, GROUPS)),
            dma((1,)),
            dma((1,)),
            dma((1,)),
            dma((NCTX,)),
            pltpu.SemaphoreType.REGULAR((ROUNDS + 1,)),
            pltpu.VMEM((ROWS, GROUP * HD), BF16),
            pltpu.SMEM((NDOCS,), jnp.int32),
            pltpu.VMEM((NCTX, NCTX), jnp.int32),
        ],
        compiler_params=pltpu.CompilerParams(
            collective_id=0, has_side_effects=True, vmem_limit_bytes=60 * 1024 * 1024
        ),
        name="attend",
    )(tokens, query, w_key, w_value, doc_lengths, balance)


def solution(mesh):
    placed = (
        P(("dp", "ctx"), "head"),
        P(("dp", "ctx"), "head"),
        P(None, "head"),
        P(None, "head"),
        P("dp"),
        P("dp", None),
    )
    return jax.shard_map(
        local, mesh=mesh, in_specs=placed, out_specs=P(("dp", "ctx"), "head"), check_vma=False
    )
```

```python
import functools

import jax
import jax.numpy as jnp
import numpy as np
from jax import lax
from jax.experimental import pallas as pl
from jax.experimental.pallas import tpu as pltpu
from jax.sharding import PartitionSpec as P

HD = 128
GROUP = 4
ROWS = 256
BROW = 8
NCTX = 32
NHEAD = 4
NDOCS = 16
FEAT = 1024
BEHIND = 8
ROPE_BASE = 500000.0
MASKED = -1e30
MESH = pl.DeviceIdType.MESH

SHIFT = 2
CHUNKS = 8
DEPTH = 4
LAG_OPP = 3

R = ROWS // CHUNKS
BACKWARD = SHIFT
FORWARD = BEHIND // 2 - SHIFT
GROUPS = CHUNKS // 2
OWN = BEHIND - 2 * SHIFT
QROWS = GROUP * ROWS
GROWS = 2 * R
PARTS = 2
BLOCK = GROUP * BROW
ROUNDS = NCTX // 4 - 1
FREQS = (ROPE_BASE ** (-(np.arange(HD // 2) * 2.0 / HD))).astype(np.float32)
EXPC = float(np.log2(np.e) / np.sqrt(HD))

F32 = jnp.float32
BF16 = jnp.bfloat16


def when(cond):
    if isinstance(cond, (bool, np.bool_)):
        return (lambda f: f()) if cond else (lambda f: None)
    return pl.when(cond)


def both(*conds):
    out = True
    for c in conds:
        if isinstance(c, (bool, np.bool_)):
            if not c:
                return False
        else:
            out = c if out is True else jnp.logical_and(out, c)
    return out


def kernel(
    tokens, query, w_key, w_value, lengths_hbm, balance_hbm, out,
    gath, wkv, part, cosf, sinf, kv, qbuf, q2, qidx, mx, tot, acc, stage, recv,
    local_sem, tsend, trecv, zsend, zrecv, srecv, qsend, qrecv, osend, orecv, round_sem, outv, lengths, balance,
):
    x = lax.axis_index("dp")
    me = lax.axis_index("ctx")
    y = lax.axis_index("head")
    z = me // 2
    core = lax.rem(me, 2)
    up = lax.rem(y + 1, NHEAD)
    down = lax.rem(y + NHEAD - 1, NHEAD)
    opposite = lax.rem(y + 2, NHEAD)
    sibling = me + 1 - 2 * core
    qshard = lax.rem(me + 2 * SHIFT, NCTX)

    def remote(src, dst, ssem, rsem, ctx, head):
        return pltpu.make_async_remote_copy(
            src_ref=src, dst_ref=dst, send_sem=ssem, recv_sem=rsem,
            device_id=(x, ctx, head), device_id_type=MESH,
        )

    def own_copy(c, p):
        rows = pl.ds(c * R, R)
        return remote(
            tokens.at[rows, :], gath.at[1 + p, rows, :], tsend.at[0], trecv.at[p, c],
            me, up if p == 0 else down,
        )

    def relay_copy(c, p):
        rows = pl.ds(c * R + p * (R // 2), R // 2)
        return remote(
            gath.at[1 + p, rows, :], gath.at[3, rows, :], tsend.at[0], trecv.at[2 + p, c],
            me, up if p == 0 else down,
        )

    def slot(u, start, size):
        return kv.at[u, pl.ds(pl.multiple_of(start, size), size), pl.ds(0, 2 * HD)]

    def hop_copy(c, sign, h):
        index = h - 1 if sign > 0 else FORWARD + h - 1
        return remote(
            slot(OWN, c * R, R), slot(OWN - sign * 2 * h, c * R, R),
            zsend.at[0], zrecv.at[index, c // 2], lax.rem(me + NCTX + sign * 2 * h, NCTX), y,
        )

    def hop_wait(g, sign, h):
        index = h - 1 if sign > 0 else FORWARD + h - 1
        here = slot(OWN - sign * 2 * h, g * GROWS, GROWS)
        pltpu.make_async_copy(here, here, zrecv.at[index, g]).wait()

    def sib_start(g, u):
        def start():
            remote(
                slot(u, g * GROWS, GROWS), slot(u - 1 + 2 * core, g * GROWS, GROWS),
                zsend.at[0], srecv.at[u // 2 - 1 + core, g], sibling, y,
            ).start()

        if u == 0:
            pl.when(core == 1)(start)
        elif u == BEHIND:
            pl.when(core == 0)(start)
        else:
            start()

    def sib_arrived(g):
        for k in range(BEHIND // 2):
            here = slot(2 * k + 1, g * GROWS, GROWS)
            pltpu.make_async_copy(here, here, srecv.at[k, g]).wait()

    def hops(g):
        sib_start(g, OWN)
        for h in range(1, max(FORWARD, BACKWARD) + 1):
            for sign, count in ((1, FORWARD), (-1, BACKWARD)):
                if h <= count:
                    hop_wait(g, sign, h)
                    sib_start(g, OWN - sign * 2 * h)

    query_copy = remote(
        query, qbuf, qsend.at[0], qrecv.at[0], lax.rem(me + NCTX - 2 * SHIFT, NCTX), y
    )

    barrier = pltpu.get_barrier_semaphore()

    ahead = lax.rem(me + 2, NCTX)
    astern = lax.rem(me + NCTX - 2, NCTX)
    for ctx, head in ((me, up), (me, down), (ahead, y), (astern, y), (sibling, y)):
        pl.semaphore_signal(barrier, inc=1, device_id=(x, ctx, head), device_id_type=MESH)

    def tell(k):
        for ctx in (ahead, astern):
            pl.semaphore_signal(
                round_sem.at[k], inc=1, device_id=(x, ctx, y), device_id_type=MESH
            )

    loads = [
        pltpu.make_async_copy(lengths_hbm, lengths, local_sem.at[4]),
        pltpu.make_async_copy(balance_hbm, balance, local_sem.at[5]),
        pltpu.make_async_copy(tokens, gath.at[0], local_sem.at[0]),
        pltpu.make_async_copy(w_value, wkv.at[:, pl.ds(0, HD)], local_sem.at[1]),
        pltpu.make_async_copy(w_key, wkv.at[:, pl.ds(HD, HD)], local_sem.at[2]),
    ]
    if SHIFT == 0:
        loads.append(pltpu.make_async_copy(query, qbuf, local_sem.at[3]))
    for load in loads:
        load.start()

    pl.semaphore_wait(barrier, 5)

    for c in range(DEPTH):
        for p in range(2):
            own_copy(c, p).start()
    tell(0)

    for load in loads[:2]:
        load.wait()
    lane = lax.broadcasted_iota(jnp.int32, (1, HD), 1)
    low = jnp.zeros((1, HD), jnp.int32)
    high = jnp.zeros((1, HD), jnp.int32)
    edge = jnp.int32(0)
    for j in range(NDOCS):
        low = jnp.where(lane == j, edge, low)
        edge = edge + lengths[j]
        high = jnp.where(lane == j, edge, high)

    def in_doc(pos):
        return (pos >= low) & (pos < high)

    pos = me * ROWS + lax.broadcasted_iota(jnp.int32, (ROWS, HD), 0)
    freq = jnp.zeros((1, HD), F32)
    for j in range(HD // 2):
        freq = jnp.where((lane & (HD // 2 - 1)) == j, float(FREQS[j]), freq)
    angle = pos.astype(F32) * freq
    cosf[...] = jnp.cos(angle)
    sine = jnp.sin(angle)
    sinf[...] = jnp.where(lax.broadcasted_iota(jnp.int32, (ROWS, HD), 1) < HD // 2, -sine, sine)

    def mark(u, carry):
        shard = (me + NCTX - BEHIND + 2 * SHIFT + u) & (NCTX - 1)
        kpos = shard * ROWS + lax.broadcasted_iota(jnp.int32, (ROWS, HD), 0)
        kv[u, :, pl.ds(2 * HD, HD)] = jnp.where(in_doc(kpos), 0.0, MASKED).astype(BF16)
        return carry

    lax.fori_loop(0, BEHIND + 1, mark, 0)
    qpos = qshard * ROWS + lax.broadcasted_iota(jnp.int32, (ROWS, HD), 0)

    mx[...] = jnp.full_like(mx, MASKED)
    tot[...] = jnp.zeros_like(tot)
    acc[...] = jnp.zeros_like(acc)
    for load in loads[2:]:
        load.wait()

    def dest_of(n, e):
        if isinstance(n, int):
            dz = 8 - n if e < 2 else (0 if n == 0 else n - 8)
        else:
            dz = 8 - n if e < 2 else jnp.where(n == 0, 0, n - 8)
        return ((z + 16 + dz) & 15) * 2 + ((core + e) & 1)

    def prepare_query():
        if SHIFT:
            query_copy.wait_recv()
        r = lax.broadcasted_iota(jnp.int32, (ROWS, NCTX), 0)
        n = r >> 5
        e = (r >> 3) & 3
        dz = jnp.where(e < 2, 8 - n, jnp.where(n == 0, 0, n - 8))
        dest = ((z + 16 + dz) & 15) * 2 + ((core + e) & 1)
        bal = balance[pl.ds(qshard, 1), :]
        pick = jnp.where(bal == dest, 1.0, 0.0).astype(BF16)
        b = lax.broadcasted_iota(jnp.int32, (NCTX, ROWS), 0)
        c = lax.broadcasted_iota(jnp.int32, (NCTX, ROWS), 1)
        widen = jnp.where((c >> 3) == b, 1.0, 0.0).astype(BF16)
        spread = jnp.dot(pick, widen, preferred_element_type=F32)
        r = lax.broadcasted_iota(jnp.int32, (ROWS, ROWS), 0)
        c = lax.broadcasted_iota(jnp.int32, (ROWS, ROWS), 1)
        perm = jnp.where((c & 7) == (r & 7), spread, 0.0).astype(BF16)
        moved = jnp.dot(perm, qbuf[...], preferred_element_type=F32)
        doc = jnp.where(in_doc(qpos), 1.0, 0.0).astype(BF16)
        doc = jnp.dot(perm, doc, preferred_element_type=F32)
        index = lax.broadcasted_iota(jnp.int32, (ROWS, HD), 0).astype(F32).astype(BF16)
        index = jnp.dot(perm, index, preferred_element_type=F32)

        def rows_of(parts):
            parts = [p.reshape(NCTX, BROW, HD) for p in parts]
            return jnp.stack(parts, axis=1).reshape(QROWS, HD)

        q2[:, pl.ds(0, HD)] = rows_of(
            [moved[:, g * HD : (g + 1) * HD] for g in range(GROUP)]
        ).astype(BF16)
        q2[:, pl.ds(HD, HD)] = rows_of([doc] * GROUP).astype(BF16)
        qidx[...] = rows_of([index] * GROUP)

    def nt(a, b):
        return lax.dot_general(a, b, (((1,), (1,)), ((), ())), preferred_element_type=F32)

    def attend(g, rows):
        group = pl.ds(g * GROWS, GROWS)
        keys = kv[pl.ds(0, BEHIND), group, pl.ds(HD, 2 * HD)].reshape(BEHIND * GROWS, 2 * HD)
        values = kv[pl.ds(0, BEHIND), group, pl.ds(0, HD)].reshape(BEHIND * GROWS, HD)
        if g % 2:
            start = g // 2 * HD
            half = pl.ds(start, HD)
            keys = jnp.concatenate([keys, kv[BEHIND, half, pl.ds(HD, 2 * HD)]], axis=0)
            values = jnp.concatenate([values, kv[BEHIND, half, pl.ds(0, HD)]], axis=0)
        score = nt(q2[rows, :], keys)
        width = score.shape[1]
        if g % 2:
            index = qidx[rows, :]
            kidx = (start + lax.broadcasted_iota(jnp.int32, index.shape, 1)).astype(F32)
            last = jnp.where(kidx <= index, score[:, width - HD :], MASKED)
            score = jnp.concatenate([score[:, : width - HD], last], axis=1)
        old = mx[rows, :]
        new = jnp.maximum(old, jnp.max(score, axis=1, keepdims=True))
        keep = jnp.exp2((old - new) * EXPC)
        weight = jnp.exp2((score - jnp.concatenate([new] * (width // HD), axis=1)) * EXPC)
        lanes = weight[:, :HD]
        for k in range(1, width // HD):
            lanes = lanes + weight[:, k * HD : (k + 1) * HD]
        mx[rows, :] = new
        tot[rows, :] = tot[rows, :] * keep + lanes
        acc[rows, :] = acc[rows, :] * keep + jnp.dot(
            weight.astype(BF16), values, preferred_element_type=F32
        )

    def out_copy(n, e):
        rows = pl.ds(pl.multiple_of((n * 4 + e) * BLOCK, BLOCK), BLOCK)
        there = pl.ds(pl.multiple_of(qshard * BLOCK, BLOCK), BLOCK)
        return remote(
            stage.at[rows, :], recv.at[there, :], osend.at[0], orecv.at[qshard],
            dest_of(n, e), y,
        )

    def finish(c):
        rows = pl.ds(c * R, R)
        for p in range(2):
            relay_copy(c, p).wait_recv()
        raw = part[rows, :] + jnp.dot(
            gath[3, rows, :], wkv[pl.ds(pl.multiple_of(opposite * FEAT, FEAT), FEAT), :],
            preferred_element_type=F32,
        )
        value = raw[:, :HD]
        key = raw[:, HD:]
        key = key * cosf[rows, :] + pltpu.roll(key, HD // 2, 1) * sinf[rows, :]
        kv[OWN, rows, pl.ds(0, 2 * HD)] = jnp.concatenate([value, key], axis=1).astype(BF16)
        for h in range(max(FORWARD, BACKWARD), 0, -1):
            for sign, count in ((1, FORWARD), (-1, BACKWARD)):
                if h <= count:
                    hop_copy(c, sign, h).start()

    def gather(i, carry):
        for p in range(2):
            own_copy(i, p).wait_recv()
            relay_copy(i, p).start()

        @pl.when(i + DEPTH < CHUNKS)
        def _():
            for p in range(2):
                own_copy(i + DEPTH, p).start()

        rows = pl.ds(i * R, R)
        total = None
        for s, source in enumerate((y, down, up)):
            term = jnp.dot(
                gath[s, rows, :], wkv[pl.ds(pl.multiple_of(source * FEAT, FEAT), FEAT), :],
                preferred_element_type=F32,
            )
            total = term if total is None else total + term
        part[rows, :] = total

        @pl.when(i >= LAG_OPP)
        def _():
            finish(i - LAG_OPP)

        @pl.when(i < ROUNDS)
        def _():
            pl.semaphore_wait(round_sem.at[i], 2)

        @pl.when(i < ROUNDS - 1)
        def _():
            tell(i + 1)

        if SHIFT:
            @pl.when(i == 0)
            def _():
                query_copy.start()

        @pl.when(i == ROUNDS)
        def _():
            pl.semaphore_signal(
                round_sem.at[ROUNDS], inc=1, device_id=(x, sibling, y), device_id_type=MESH
            )
            pl.semaphore_wait(round_sem.at[ROUNDS], 1)

        return carry

    lax.fori_loop(0, CHUNKS, gather, 0)
    def finish_loop(c, carry):
        finish(c)
        return carry

    every = pl.ds(0, QROWS)
    lax.fori_loop(CHUNKS - LAG_OPP, CHUNKS - 1, finish_loop, 0)
    hops(0)
    prepare_query()
    finish(CHUNKS - 1)
    hops(1)
    sib_arrived(0)
    attend(0, every)
    hops(2)
    sib_arrived(1)
    attend(1, every)
    hops(3)
    sib_arrived(2)
    attend(2, every)
    sib_arrived(3)

    def send(rb, carry):
        for e in range(4):
            if e == 2:
                @pl.when(rb > 0)
                def _():
                    out_copy(rb, e).start()
            else:
                out_copy(rb, e).start()
        return carry

    for p in range(PARTS):
        rows = pl.ds(p * (QROWS // PARTS), QROWS // PARTS)
        attend(3, rows)
        total = jnp.sum(tot[rows, :], axis=1, keepdims=True)
        stage[rows, :] = (acc[rows, :] / total).astype(BF16)
        lax.fori_loop(p * (8 // PARTS), (p + 1) * (8 // PARTS), send, 0)

    def sent(block, sem):
        pltpu.make_async_copy(block, block, sem).wait()

    sent(gath.at[pl.ds(0, 3)], tsend.at[0])
    sent(gath.at[pl.ds(0, 2)], zsend.at[0])
    if SHIFT:
        query_copy.wait_send()

    def arrive(dz, own):
        source = (z + 16 + dz) & 15
        chip = (source + SHIFT) & 15
        for k in range(2):
            shard = chip * 2 + k
            there = pl.ds(pl.multiple_of(shard * BLOCK, BLOCK), BLOCK)

            def landed():
                remote(
                    stage.at[pl.ds(0, BLOCK), :], recv.at[there, :], osend.at[0], orecv.at[shard],
                    sibling, y,
                ).wait_recv()

            if own:
                pl.when(core != k)(landed)
            else:
                landed()
        if own:
            there = pl.ds(pl.multiple_of(qshard * BLOCK, BLOCK), BLOCK)
            recv[there, :] = stage[pl.ds(2 * BLOCK, BLOCK), :]
        block = recv[pl.ds(pl.multiple_of(chip * 2 * BLOCK, 2 * BLOCK), 2 * BLOCK), :].astype(F32)
        heads = [
            jnp.concatenate(
                [
                    block[g * BROW : (g + 1) * BROW],
                    block[BLOCK + g * BROW : BLOCK + (g + 1) * BROW],
                ],
                axis=0,
            )
            for g in range(GROUP)
        ]
        final = pl.ds(pl.multiple_of(chip * 2 * BROW, 2 * BROW), 2 * BROW)
        outv[final, :] = jnp.concatenate(heads, axis=1).astype(BF16)
        pltpu.make_async_copy(outv.at[final, :], out.at[final, :], local_sem.at[3]).start()

    arrive(0, True)
    arrive(8, False)

    def pair(n, carry):
        arrive(8 - n, False)
        arrive(n - 8, False)
        return carry

    lax.fori_loop(1, 8, pair, 0)

    sent(stage.at[pl.ds(0, QROWS - BLOCK), :], osend.at[0])
    sent(outv, local_sem.at[3])


def local(tokens, query, w_key, w_value, doc_lengths, balance):
    hbm = pl.BlockSpec(memory_space=pltpu.HBM)
    dma = pltpu.SemaphoreType.DMA
    width = 2 * HD
    return pl.pallas_call(
        kernel,
        out_shape=jax.ShapeDtypeStruct((ROWS, GROUP * HD), BF16),
        in_specs=[hbm] * 6,
        out_specs=hbm,
        scratch_shapes=[
            pltpu.VMEM((NHEAD, ROWS, FEAT), BF16),
            pltpu.VMEM((NHEAD * FEAT, width), BF16),
            pltpu.VMEM((ROWS, width), F32),
            pltpu.VMEM((ROWS, HD), F32),
            pltpu.VMEM((ROWS, HD), F32),
            pltpu.VMEM((BEHIND + 1, ROWS, 3 * HD), BF16),
            pltpu.VMEM((ROWS, GROUP * HD), BF16),
            pltpu.VMEM((QROWS, width), BF16),
            pltpu.VMEM((QROWS, HD), F32),
            pltpu.VMEM((QROWS, HD), F32),
            pltpu.VMEM((QROWS, HD), F32),
            pltpu.VMEM((QROWS, HD), F32),
            pltpu.VMEM((QROWS, HD), BF16),
            pltpu.VMEM((QROWS, HD), BF16),
            dma((6,)),
            dma((1,)),
            dma((4, CHUNKS)),
            dma((1,)),
            dma((FORWARD + BACKWARD, GROUPS)),
            dma((BEHIND // 2, GROUPS)),
            dma((1,)),
            dma((1,)),
            dma((1,)),
            dma((NCTX,)),
            pltpu.SemaphoreType.REGULAR((ROUNDS + 1,)),
            pltpu.VMEM((ROWS, GROUP * HD), BF16),
            pltpu.SMEM((NDOCS,), jnp.int32),
            pltpu.VMEM((NCTX, NCTX), jnp.int32),
        ],
        compiler_params=pltpu.CompilerParams(
            collective_id=0, has_side_effects=True, vmem_limit_bytes=60 * 1024 * 1024
        ),
        name="attend",
    )(tokens, query, w_key, w_value, doc_lengths, balance)


def solution(mesh):
    placed = (
        P(("dp", "ctx"), "head"),
        P(("dp", "ctx"), "head"),
        P(None, "head"),
        P(None, "head"),
        P("dp"),
        P("dp", None),
    )
    return jax.shard_map(
        local, mesh=mesh, in_specs=placed, out_specs=P(("dp", "ctx"), "head"), check_vma=False
    )
```
